256 devices in a mesh: tm: 8 (over x, core), cohort: 32 (over z, y).
Axes of the slice: x: 4, y: 4, z: 8, core: 2. Of those that a mesh axis runs over, the one named last changes fastest.
Arguments:
- transition: float32 [64, 64, 256, 256], P('tm', 'cohort'), may hold values from 0 to 1, as said below
- entry: int32 [64], P('cohort'), may hold values from 0 to 63, as said below
- share: float32 [64], P('cohort'), may hold values from 0.1 to 1
Outputs:
- cumulative: float32 [64, 64, 256, 256], P('tm', 'cohort')
- pooled: float32 [64, 256, 256], P('tm', 'cohort')
The draws below stay inside these ranges and needn't reach their ends.
Inputs may be any that keep to these rules, and one draw needn't show every extreme that they name: `entry`: month numbers within the window; some group enters at month 0 and some at the window's last month. `transition`: each row of every monthly matrix is nonnegative and sums to one, with a diagonal entry of at least 0.7.
All inputs are finite; a program needn't handle non-finite values.
Results may differ from the reference program's by a relative error of at most 0.0001.
Values sent between devices are 32-bit elements; how exact they have to be, the bound alone decides.
A program may use at most 64 MiB of HBM per device.

```python
import math
import jax
import jax.numpy as jnp
from jax import lax

NS = 256
MONTHS = 64
GROUPS = 64


def draw_transition(key, part):
    keys = jax.random.split(jax.random.fold_in(key, 11), 4)
    diag_low, diag_high, widest, power, far_power, far_share = (0.7, 0.8, 8, 1.0, 24.0, 0.5)
    diag_part = jax.random.uniform(keys[0], (MONTHS, GROUPS, NS, 1), jnp.float32, diag_low, diag_high)
    reach = jax.random.randint(keys[1], (MONTHS, GROUPS, NS, 1), 1, widest + 1)
    row_index = jnp.arange(NS)[:, None]
    column_index = jnp.arange(NS)[None, :]
    distance = jnp.abs(row_index - column_index)
    in_band = (distance >= 1) & (distance <= reach)
    raw_band = jax.random.uniform(keys[2], (MONTHS, GROUPS, NS, NS), jnp.float32, 0.0, 1.0) ** power + 0.001
    band = jnp.where(in_band, raw_band, 0.0)
    band = band / jnp.sum(band, axis=-1, keepdims=True)
    unit = jnp.eye(NS, dtype=jnp.float32)
    raw_far = jax.random.uniform(keys[3], (MONTHS, GROUPS, NS, NS), jnp.float32, 0.0, 1.0) ** far_power + 0.001
    far_part = raw_far * (1.0 - unit)
    far_part = far_part / jnp.sum(far_part, axis=-1, keepdims=True)
    off_part = (1.0 - diag_part) * ((1.0 - far_share) * band + far_share * far_part)
    return (off_part + diag_part * unit).astype(jnp.float32)


def draw_entry(key, part):
    base_key, pick_key = jax.random.split(jax.random.fold_in(key, 23))
    values = jax.random.randint(base_key, (GROUPS,), 0, MONTHS)
    picks = jax.random.permutation(pick_key, GROUPS)
    values = values.at[picks[0]].set(0)
    values = values.at[picks[1]].set(MONTHS - 1)
    return values.astype(jnp.int32)


def shard_levels(stream_key, dims, shards, low, top_value):
    loudness = 1.0
    for axis_at, shards_of in shards:
        draws = jax.random.uniform(jax.random.fold_in(jax.random.fold_in(stream_key, 6), axis_at), (shards_of,), jnp.float32, low / len(shards), top_value / len(shards))
        loudness = loudness * jnp.repeat(jnp.exp(draws), dims[axis_at] // shards_of).reshape((-1,) + (1,) * (len(dims) - 1 - axis_at))
    return loudness


def setup_inputs(seed: int = 0) -> dict:
    streams_of = jax.random.split(jax.random.key(seed), 4)
    return {
        "transition": draw_transition(jax.random.fold_in(streams_of[3], 71), 0),
        "entry": draw_entry(jax.random.fold_in(streams_of[3], 71), 0),
        "share": jnp.clip(jnp.exp(math.log(1.0) - 2.3025851 * jax.random.uniform(streams_of[2], (GROUPS,), jnp.float32) ** shard_levels(streams_of[2], (GROUPS,), ((0, 32),), -0.2, 0.2)), 0.1, 1.0),
    }


kernel_weights = (1.0 / 16, 2.0 / 16, 3.0 / 16, 4.0 / 16, 3.0 / 16, 2.0 / 16, 1.0 / 16)


def reference(transition, entry, share):
    months_all = transition.shape[0]
    states = transition.shape[2]
    padded = jnp.pad(transition, ((3, 3), (0, 0), (0, 0), (0, 0)))
    month_idx = jnp.arange(months_all).astype(jnp.int32)
    smoothed = jnp.zeros_like(transition)
    weight_sum = jnp.zeros((months_all,), transition.dtype)
    for offset in range(7):
        smoothed = smoothed + kernel_weights[offset] * padded[offset:offset + months_all]
        inside = (month_idx + offset - 3 >= 0) & (month_idx + offset - 3 < months_all)
        weight_sum = weight_sum + jnp.where(inside, kernel_weights[offset], 0.0).astype(transition.dtype)
    graduated = smoothed / weight_sum[:, None, None, None]
    unit = jnp.eye(states, dtype=transition.dtype)
    active = month_idx[:, None] >= entry[None, :]
    monthly = jnp.where(active[:, :, None, None], graduated, unit)

    def advance(running, matrix):
        nxt = jnp.einsum("gij,gjk->gik", running, matrix, precision=lax.Precision.HIGHEST)
        summed = jnp.einsum("g,gij->ij", share, nxt, precision=lax.Precision.HIGHEST)
        return nxt, (nxt, summed)

    start_state = jnp.broadcast_to(unit, transition.shape[1:])
    _, (cumulative, pooled) = lax.scan(advance, start_state, monthly)
    return cumulative, pooled
```

```python
import functools

import jax
import jax.numpy as jnp
from jax import lax
from jax.experimental import pallas as pl
from jax.experimental.pallas import tpu as pltpu
from jax.sharding import PartitionSpec as P

MESH = pl.DeviceIdType.MESH
F32 = jnp.float32
BF16 = jnp.bfloat16
VMEM_LIMIT = 56 * 1024 * 1024


def ring_places(nz):
    half = nz // 2
    plus = [(p, 0) for p in range(half)] + [(p, 1) for p in range(half - 2, -1, -1)]
    minus = [(p, 1) for p in range(half - 1)] + [(half - 1, 0)] + [(p, 0) for p in range(half - 2, -1, -1)]
    return plus, minus


def kernel(
    nz, ny, trans, entry, share, cum_out, pooled,
    own, hp, hn, mon, pre, t0s, t0r, t0b, carry, cab, cum, wa, wb, ra, rb, rya, ryb,
    own_sem, fs_sem, bs_sem, hp_sem, hn_sem, t0_sem, cs_sem, cr_sem, cf_sem, out_sem,
    as_sem, ar_sem, bzs_sem, bzr_sem, yas_sem, yar_sem, ybs_sem, ybr_sem,
):
    n = own.shape[-1]
    pairs = nz // 2
    rows = n // nz
    sub = rows // ny
    block = 2 * rows
    tm = lax.axis_index("tm")
    co = lax.axis_index("cohort")
    ntm = lax.axis_size("tm")
    core, chip = lax.rem(tm, 2), tm // 2
    z, y = co // ny, lax.rem(co, ny)
    has_prev, has_next = tm > 0, tm < ntm - 1
    first_chip, last_chip = chip == 0, chip == ntm // 2 - 1
    z_up = lax.rem(z + 1, nz) * ny + y
    z_down = lax.rem(z + nz - 1, nz) * ny + y

    def y_peer(o):
        return lax.rem(y + o, ny)

    barrier = pltpu.get_barrier_semaphore()

    def greet(t, c):
        pl.semaphore_signal(barrier, inc=1, device_id=(t, c), device_id_type=MESH)

    near = (
        (has_prev, tm - 1), (has_next, tm + 1),
        ((core == 1) & (tm > 1), tm - 2), ((core == 1) & (tm < ntm - 2), tm + 2),
    )
    peers = 1 + ny
    for cond, t in near:
        pl.when(cond)(functools.partial(greet, t, co))
        peers = peers + jnp.where(cond, 1, 0)
    for c in [z_up, z_down] + [z * ny + y_peer(o) for o in range(1, ny)]:
        greet(tm, c)
    pl.semaphore_wait(barrier, peers)

    def remote(src, dst, ss, rs, t, c):
        return pltpu.make_async_remote_copy(
            src_ref=src, dst_ref=dst, send_sem=ss, recv_sem=rs, device_id=(t, c), device_id_type=MESH
        )

    def fwd_halo(i):
        return remote(trans.at[5 + i], hp.at[i], fs_sem.at[i], hp_sem.at[i], tm + 1, co)

    def bwd_halo(i):
        return remote(trans.at[i], hn.at[i], bs_sem.at[i], hn_sem.at[i], tm - 1, co)

    def own_copy(i):
        return pltpu.make_async_copy(trans.at[i], own.at[i], own_sem.at[i])

    @pl.when(has_next)
    def _():
        for i in (2, 1, 0):
            fwd_halo(i).start()

    @pl.when(has_prev)
    def _():
        for i in (0, 1, 2):
            bwd_halo(i).start()

    for i in range(8):
        own_copy(i).start()

    @pl.when(jnp.logical_not(has_prev))
    def _():
        hp[...] = jnp.zeros_like(hp)

    @pl.when(jnp.logical_not(has_next))
    def _():
        hn[...] = jnp.zeros_like(hn)

    strip = min(64, n)

    def graduate(t):
        def at(e):
            return (hp, e + 3) if e < 0 else ((hn, e - 8) if e > 7 else (own, e))

        edge = {0: 10, 1: 13, 2: 15, 5: 15, 6: 13, 7: 10}.get(t)
        scale = 1.0 / 16
        if edge is not None:
            scale = jnp.where(tm == (0 if t < 3 else ntm - 1), F32(1.0 / edge), F32(1.0 / 16))

        def step(i, _):
            g, r0 = i // (n // strip), pl.multiple_of(lax.rem(i, n // strip) * strip, strip)
            act = jnp.where(8 * tm + t >= entry[g], F32(1.0), F32(0.0))

            def load(e):
                ref, k = at(e)
                return ref[k, g, pl.ds(r0, strip), :]

            total = (
                4.0 * load(t) + 3.0 * (load(t - 1) + load(t + 1))
                + 2.0 * (load(t - 2) + load(t + 2)) + (load(t - 3) + load(t + 3))
            )
            row = lax.broadcasted_iota(jnp.int32, (strip, n), 0) + r0
            col = lax.broadcasted_iota(jnp.int32, (strip, n), 1)
            unit = jnp.where(row == col, 1.0 - act, 0.0)
            v = total * (act * scale) + unit
            hi = v.astype(BF16)
            mon[t, g, 0, pl.ds(r0, strip), :] = hi
            mon[t, g, 1, pl.ds(r0, strip), :] = (v - hi.astype(F32)).astype(BF16)
            return 0

        lax.fori_loop(0, 2 * (n // strip), step, 0)

    def dot(a, b):
        return jnp.dot(a, b, preferred_element_type=F32)

    def times(a, b):
        r = a.shape[1]
        both = dot(a.reshape(2 * r, n), b[0])
        return both[:r] + both[r:] + dot(a[0], b[1])

    def halves(ref, v):
        hi = v.astype(BF16)
        ref[0] = hi
        ref[1] = (v - hi.astype(F32)).astype(BF16)

    def multiply(dst, a, b, keep=None):
        def step(g, _):
            v = times(a(g), b(g))
            halves(pre.at[dst, g], v)
            if keep is not None:
                keep[g] = v
            return 0
        lax.fori_loop(0, 2, step, 0)

    def take(ref, k):
        return lambda g: ref[k, g]

    def copy_pre(t):
        pre[t] = mon[t]

    def fwd_wait(i):
        pl.when(has_prev)(lambda: fwd_halo(i).wait_recv())

    def bwd_wait(i):
        pl.when(has_next)(lambda: bwd_halo(i).wait_recv())

    for i in range(8):
        own_copy(i).wait()
    graduate(3)
    graduate(4)

    def send_t0():
        return remote(t0s, t0r, t0_sem.at[0], t0_sem.at[1], tm + 1, co)

    @pl.when(core == 0)
    def _():
        for i in range(3):
            bwd_wait(i)
            graduate(5 + i)
        copy_pre(3)
        for t in range(4, 8):
            multiply(t, take(pre, t - 1), take(mon, t))
        fwd_wait(2)
        graduate(2)
        fwd_wait(1)
        graduate(1)
        copy_pre(1)
        multiply(2, take(mon, 1), take(mon, 2))
        for t in range(3, 8):
            multiply(t, take(pre, 2), take(pre, t))
        fwd_wait(0)
        graduate(0)
        multiply(7, take(mon, 0), take(pre, 7), t0s)
        send_t0().start()
        for t in range(6, 0, -1):
            multiply(t, take(mon, 0), take(pre, t))
        copy_pre(0)

    @pl.when(core == 1)
    def _():
        for i in (2, 1, 0):
            fwd_wait(i)
            graduate(i)
        copy_pre(0)
        for t in range(1, 5):
            multiply(t, take(pre, t - 1), take(mon, t))
        for t in range(5, 8):
            bwd_wait(t - 5)
            graduate(t)
            multiply(t, take(pre, t - 1), take(mon, t))
        send_t0().wait_recv()
        for g in range(2):
            halves(t0b.at[g], t0r[g])
        for t in range(7, -1, -1):
            multiply(t, lambda g: t0b[g], take(pre, t))

    def chunk(p, side):
        if p == pairs - 1:
            return lax.rem(z + nz - pairs, nz) if side == 0 else z
        return lax.rem(z + nz - 1 - p, nz) if side == 0 else lax.rem(z + 1 + p, nz)

    def carry_on(p):
        return remote(cum.at[p, 7], carry.at[p], cs_sem.at[p], cr_sem.at[p], tm + 2, co)

    def carry_back(p):
        return remote(carry.at[p], carry.at[p], cf_sem.at[p], cr_sem.at[p], tm - 1, co)

    def out_copy(p, side):
        return pltpu.make_async_copy(
            cum.at[p, :, :, pl.ds(side * rows, rows), :],
            cum_out.at[:, :, pl.ds(pl.multiple_of(chunk(p, side) * rows, rows), rows), :],
            out_sem.at[p, side],
        )

    def advance(p, t):
        total = None
        for g in range(2):
            v = times(cab[g], pre[t, g])
            cum[p, t, g] = v
            w = share[g] * v
            total = w if total is None else total + w
        return total

    plus, minus = ring_places(nz)
    places = (plus, minus)
    targets = (z_up, z_down)

    def a_copy(d, s):
        p, side = places[d][s]
        src = wa.at[p, pl.ds(2 * d, 2), pl.ds(side * rows, rows), :] if s == 0 else ra.at[d, s - 1]
        return remote(src, ra.at[d, s], as_sem.at[d, s], ar_sem.at[d, s], tm, targets[d])

    def a_step(d, s):
        p, side = places[d][s]
        if s > 0:
            a_copy(d, s - 1).wait_recv()
            ra[d, s - 1] += wa[p, 2 * d : 2 * d + 2, side * rows : (side + 1) * rows, :]
        a_copy(d, s).start()

    def yb_copy(p, side, o):
        src = wb.at[p, :, pl.ds(pl.multiple_of(side * rows + y_peer(o) * sub, sub), sub), :]
        k = 2 * p + side
        return remote(
            src, ryb.at[k, o - 1], ybs_sem.at[k, o - 1], ybr_sem.at[k, o - 1], tm, z * ny + y_peer(o)
        )

    def yb_sum(d, p, side):
        v = wb[p, 2 * d : 2 * d + 2, pl.ds(pl.multiple_of(side * rows + y * sub, sub), sub), :]
        for o in range(1, ny):
            v = v + ryb[2 * p + side, o - 1, 2 * d : 2 * d + 2]
        return v

    got = set()

    def yb_wait(p, side):
        if (p, side) not in got:
            got.add((p, side))
            for o in range(1, ny):
                yb_copy(p, side, o).wait_recv()

    def b_copy(d, s):
        return remote(rb.at[d, s], rb.at[d, s + 1], bzs_sem.at[d, s], bzr_sem.at[d, s], tm, targets[d])

    def b_step(d, s):
        p, side = places[d][s]
        yb_wait(p, side)
        v = yb_sum(d, p, side)
        if s > 0:
            b_copy(d, s - 1).wait_recv()
            rb[d, s] += v
        else:
            rb[d, 0] = v
        b_copy(d, s).start()

    for p in range(pairs):
        @pl.when(first_chip)
        def _():
            row = lax.broadcasted_iota(jnp.int32, (rows, n), 0)
            col = lax.broadcasted_iota(jnp.int32, (rows, n), 1)
            for side in range(2):
                unit = jnp.where(row + chunk(p, side) * rows == col, F32(1.0), F32(0.0))
                for g in range(2):
                    carry[p, g, side * rows : (side + 1) * rows, :] = unit

        @pl.when(jnp.logical_not(first_chip) & (core == 1))
        def _():
            carry_on(p).wait_recv()
            carry_back(p).start()

        @pl.when(jnp.logical_not(first_chip) & (core == 0))
        def _():
            carry_back(p).wait_recv()

        for g in range(2):
            halves(cab.at[g], carry[p, g])
        wb[p, 3] = advance(p, 7)
        pl.when((core == 1) & jnp.logical_not(last_chip))(lambda: carry_on(p).start())

        def b_month(t, _):
            wb[p, t] = advance(p, t + 4)
            return 0

        lax.fori_loop(0, 3, b_month, 0)
        for side in range(2):
            for o in range(1, ny):
                yb_copy(p, side, o).start()

        def a_month(t, _):
            wa[p, t] = advance(p, t)
            return 0

        lax.fori_loop(0, 4, a_month, 0)
        for side in range(2):
            out_copy(p, side).start()
        for d in range(2):
            a_step(d, p)
        if p > 0:
            for d in range(2):
                b_step(d, p - 1)

    last = (pairs - 1, 1)
    for s in range(pairs, nz - 1):
        for d in range(2):
            a_step(d, s)
        for d in range(2):
            b_step(d, s - 1)

    for d in range(2):
        a_copy(d, nz - 2).wait_recv()
        ra[d, nz - 2] += wa[last[0], 2 * d : 2 * d + 2, rows : 2 * rows, :]

    def ya_copy(d, o):
        src = ra.at[d, nz - 2, :, pl.ds(pl.multiple_of(y_peer(o) * sub, sub), sub), :]
        return remote(
            src, rya.at[d, o - 1], yas_sem.at[d, o - 1], yar_sem.at[d, o - 1], tm, z * ny + y_peer(o)
        )

    for d in range(2):
        for o in range(1, ny):
            ya_copy(d, o).start()
    for d in range(2):
        b_step(d, nz - 2)
    yb_wait(*last)
    for d in range(2):
        v = yb_sum(d, *last)
        b_copy(d, nz - 2).wait_recv()
        pooled[4 + 2 * d : 6 + 2 * d] = v + rb[d, nz - 1]
    for d in range(2):
        v = ra[d, nz - 2, :, pl.ds(pl.multiple_of(y * sub, sub), sub), :]
        for o in range(1, ny):
            ya_copy(d, o).wait_recv()
            v = v + rya[d, o - 1]
        pooled[2 * d : 2 * d + 2] = v

    for i in range(3):
        pl.when(has_next)(lambda: fwd_halo(i).wait_send())
        pl.when(has_prev)(lambda: bwd_halo(i).wait_send())
    pl.when(core == 0)(lambda: send_t0().wait_send())
    for p in range(pairs):
        pl.when((core == 1) & jnp.logical_not(last_chip))(lambda: carry_on(p).wait_send())
        pl.when((core == 1) & jnp.logical_not(first_chip))(lambda: carry_back(p).wait_send())
        for side in range(2):
            out_copy(p, side).wait()
            for o in range(1, ny):
                yb_copy(p, side, o).wait_send()
    for d in range(2):
        for s in range(nz - 1):
            a_copy(d, s).wait_send()
            b_copy(d, s).wait_send()
        for o in range(1, ny):
            ya_copy(d, o).wait_send()


def on_device(nz, ny, transition, entry, share):
    n = transition.shape[-1]
    pairs, rows = nz // 2, n // nz
    sub = rows // ny
    dma = pltpu.SemaphoreType.DMA
    return pl.pallas_call(
        functools.partial(kernel, nz, ny),
        out_shape=(
            jax.ShapeDtypeStruct(transition.shape, F32),
            jax.ShapeDtypeStruct((8, sub, n), F32),
        ),
        in_specs=[
            pl.BlockSpec(memory_space=pl.ANY),
            pl.BlockSpec(memory_space=pltpu.SMEM),
            pl.BlockSpec(memory_space=pltpu.SMEM),
        ],
        out_specs=(pl.BlockSpec(memory_space=pl.ANY), pl.BlockSpec(memory_space=pltpu.VMEM)),
        scratch_shapes=[
            pltpu.VMEM((8, 2, n, n), F32),
            pltpu.VMEM((3, 2, n, n), F32),
            pltpu.VMEM((3, 2, n, n), F32),
            pltpu.VMEM((8, 2, 2, n, n), BF16),
            pltpu.VMEM((8, 2, 2, n, n), BF16),
            pltpu.VMEM((2, n, n), F32),
            pltpu.VMEM((2, n, n), F32),
            pltpu.VMEM((2, 2, n, n), BF16),
            pltpu.VMEM((pairs, 2, 2 * rows, n), F32),
            pltpu.VMEM((2, 2, 2 * rows, n), BF16),
            pltpu.VMEM((pairs, 8, 2, 2 * rows, n), F32),
            pltpu.VMEM((pairs, 4, 2 * rows, n), F32),
            pltpu.VMEM((pairs, 4, 2 * rows, n), F32),
            pltpu.VMEM((2, nz - 1, 2, rows, n), F32),
            pltpu.VMEM((2, nz, 2, sub, n), F32),
            pltpu.VMEM((2, ny - 1, 2, sub, n), F32),
            pltpu.VMEM((nz, ny - 1, 4, sub, n), F32),
            dma((8,)), dma((3,)), dma((3,)), dma((3,)), dma((3,)), dma((2,)),
            dma((pairs,)), dma((pairs,)), dma((pairs,)), dma((pairs, 2)),
            dma((2, nz - 1)), dma((2, nz - 1)), dma((2, nz - 1)), dma((2, nz - 1)),
            dma((2, ny - 1)), dma((2, ny - 1)), dma((nz, ny - 1)), dma((nz, ny - 1)),
        ],
        compiler_params=pltpu.CompilerParams(
            collective_id=0, has_side_effects=True, vmem_limit_bytes=VMEM_LIMIT
        ),
        cost_estimate=pl.CostEstimate(
            flops=3 * 2 * 46 * n**3, bytes_accessed=2 * 4 * 16 * n * n, transcendentals=0
        ),
    )(transition, entry, share)


def solution(mesh, nz=8, ny=4):
    return jax.shard_map(
        functools.partial(on_device, nz, ny),
        mesh=mesh,
        in_specs=(P("tm", "cohort", None, None), P("cohort"), P("cohort")),
        out_specs=(P("tm", "cohort", None, None), P("tm", "cohort", None)),
        check_vma=False,
    )
```

```python
import functools

import jax
import jax.numpy as jnp
from jax import lax
from jax.experimental import pallas as pl
from jax.experimental.pallas import tpu as pltpu
from jax.sharding import PartitionSpec as P

MESH = pl.DeviceIdType.MESH
F32 = jnp.float32
BF16 = jnp.bfloat16
OUT = pltpu.VMEM
VMEM_LIMIT = 48 * 1024 * 1024


def chunk_order(nz):
    half = nz // 2
    far = [half]
    for d in range(half - 1, 0, -1):
        far += [d, -d]
    return far + [0]


def chunk_blocks(nz):
    sizes = [1] + [2] * (nz // 2 - 2) + [3]
    starts = [sum(sizes[:i]) for i in range(len(sizes))]
    return [list(range(a, a + m)) for a, m in zip(starts, sizes)]


def kernel(
    nz, ny, trans, entry, share, cum_out, pooled,
    own, hp, hn, mon, pre, t0s, t0r, late, qs, qb, carry, outc, cab, wa, wb, ra, rb, rya, ryb,
    own_sem, fs_sem, bs_sem, hp_sem, hn_sem, t0_sem, cs_sem, cr_sem, cf_sem,
    as_sem, ar_sem, bzs_sem, bzr_sem, yas_sem, yar_sem, ybs_sem, ybr_sem,
):
    n = own.shape[-1]
    half = nz // 2
    rows = n // nz
    sub = rows // ny
    order = chunk_order(nz)
    tm = lax.axis_index("tm")
    co = lax.axis_index("cohort")
    ntm = lax.axis_size("tm")
    core, chip = lax.rem(tm, 2), tm // 2
    z, y = co // ny, lax.rem(co, ny)
    has_prev, has_next = tm > 0, tm < ntm - 1
    first_chip, last_chip = chip == 0, chip == ntm // 2 - 1
    z_up = lax.rem(z + 1, nz) * ny + y
    z_down = lax.rem(z + nz - 1, nz) * ny + y

    def y_peer(o):
        return lax.rem(y + o, ny)

    barrier = pltpu.get_barrier_semaphore()

    def greet(t, c):
        pl.semaphore_signal(barrier, inc=1, device_id=(t, c), device_id_type=MESH)

    near = (
        (has_prev, tm - 1), (has_next, tm + 1),
        ((core == 1) & (tm > 1), tm - 2), ((core == 1) & (tm < ntm - 2), tm + 2),
    )
    peers = 1 + ny
    for cond, t in near:
        pl.when(cond)(functools.partial(greet, t, co))
        peers = peers + jnp.where(cond, 1, 0)
    for c in [z_up, z_down] + [z * ny + y_peer(o) for o in range(1, ny)]:
        greet(tm, c)
    pl.semaphore_wait(barrier, peers)

    def remote(src, dst, ss, rs, t, c):
        return pltpu.make_async_remote_copy(
            src_ref=src, dst_ref=dst, send_sem=ss, recv_sem=rs, device_id=(t, c), device_id_type=MESH
        )

    def fwd_halo(i):
        return remote(trans.at[5 + i], hp.at[i], fs_sem.at[i], hp_sem.at[i], tm + 1, co)

    def bwd_halo(i):
        return remote(trans.at[i], hn.at[i], bs_sem.at[i], hn_sem.at[i], tm - 1, co)

    def own_copy(i):
        return pltpu.make_async_copy(trans.at[i], own.at[i], own_sem.at[i])

    @pl.when(has_next)
    def _():
        for i in (2, 1, 0):
            fwd_halo(i).start()

    @pl.when(has_prev)
    def _():
        for i in (0, 1, 2):
            bwd_halo(i).start()

    for i in range(8):
        own_copy(i).start()

    @pl.when(jnp.logical_not(has_prev))
    def _():
        hp[...] = jnp.zeros_like(hp)

    @pl.when(jnp.logical_not(has_next))
    def _():
        hn[...] = jnp.zeros_like(hn)

    strip = min(64, n)

    def graduate(t):
        def at(e):
            return (hp, e + 3) if e < 0 else ((hn, e - 8) if e > 7 else (own, e))

        edge = {0: 10, 1: 13, 2: 15, 5: 15, 6: 13, 7: 10}.get(t)
        scale = 1.0 / 16
        if edge is not None:
            scale = jnp.where(tm == (0 if t < 3 else ntm - 1), F32(1.0 / edge), F32(1.0 / 16))

        def step(i, _):
            g, r0 = i // (n // strip), pl.multiple_of(lax.rem(i, n // strip) * strip, strip)
            act = jnp.where(8 * tm + t >= entry[g], F32(1.0), F32(0.0))

            def load(e):
                ref, k = at(e)
                return ref[k, g, pl.ds(r0, strip), :]

            total = (
                4.0 * load(t) + 3.0 * (load(t - 1) + load(t + 1))
                + 2.0 * (load(t - 2) + load(t + 2)) + (load(t - 3) + load(t + 3))
            )
            row = lax.broadcasted_iota(jnp.int32, (strip, n), 0) + r0
            col = lax.broadcasted_iota(jnp.int32, (strip, n), 1)
            unit = jnp.where(row == col, 1.0 - act, 0.0)
            v = total * (act * scale) + unit
            hi = v.astype(BF16)
            mon[t, g, 0, pl.ds(r0, strip), :] = hi
            mon[t, g, 1, pl.ds(r0, strip), :] = (v - hi.astype(F32)).astype(BF16)
            return 0

        lax.fori_loop(0, 2 * (n // strip), step, 0)

    def dot(a, b):
        return jnp.dot(a, b, preferred_element_type=F32)

    def times(a, b):
        r = a.shape[1]
        both = dot(a.reshape(2 * r, n), b[0])
        return both[:r] + both[r:] + dot(a[0], b[1])

    def halves(ref, v):
        hi = v.astype(BF16)
        ref[0] = hi
        ref[1] = (v - hi.astype(F32)).astype(BF16)

    def multiply(dst, a, b, keep=None):
        def step(g, _):
            v = times(a(g), b(g))
            halves(dst.at[g], v)
            if keep is not None:
                keep[g] = v
            return 0
        lax.fori_loop(0, 2, step, 0)

    def take(ref, k):
        return lambda g: ref[k, g]

    def copy_pre(t):
        pre[t] = mon[t]

    def fwd_wait(i):
        pl.when(has_prev)(lambda: fwd_halo(i).wait_recv())

    def bwd_wait(i):
        pl.when(has_next)(lambda: bwd_halo(i).wait_recv())

    for i in range(8):
        own_copy(i).wait()
    graduate(3)
    graduate(4)

    def send_t0():
        return remote(t0s, t0r, t0_sem.at[0], t0_sem.at[1], tm + 1, co)

    @pl.when(core == 0)
    def _():
        for i in range(3):
            bwd_wait(i)
            graduate(5 + i)
        copy_pre(3)
        for t in range(4, 8):
            multiply(pre.at[t], take(pre, t - 1), take(mon, t))
        fwd_wait(2)
        graduate(2)
        fwd_wait(1)
        graduate(1)
        copy_pre(1)
        multiply(pre.at[2], take(mon, 1), take(mon, 2))
        for t in range(3, 8):
            multiply(pre.at[t], take(pre, 2), take(pre, t))
        row = lax.broadcasted_iota(jnp.int32, (n, n), 0)
        col = lax.broadcasted_iota(jnp.int32, (n, n), 1)
        for g in range(2):
            halves(pre.at[0, g], jnp.where(row == col, F32(1.0), F32(0.0)))
        fwd_wait(0)
        graduate(0)
        multiply(qb, take(mon, 0), take(pre, 7), t0s)
        send_t0().start()
        late[...] = mon[0]

    @pl.when(core == 1)
    def _():
        for i in (2, 1, 0):
            fwd_wait(i)
            graduate(i)
        copy_pre(0)
        for t in range(1, 5):
            multiply(pre.at[t], take(pre, t - 1), take(mon, t))
        for t in range(5, 8):
            bwd_wait(t - 5)
            graduate(t)
            multiply(pre.at[t], take(pre, t - 1), take(mon, t))
        send_t0().wait_recv()
        for g in range(2):
            halves(late.at[g], t0r[g])
        pl.when(jnp.logical_not(last_chip))(
            lambda: multiply(qb, lambda g: late[g], take(pre, 7), qs)
        )

    def chunk(j):
        return lax.rem(z + nz + order[j], nz)

    def chunk_rows(j):
        return pl.ds(pl.multiple_of(chunk(j) * rows, rows), rows)

    def carry_on(j, first):
        src = qs.at[:, chunk_rows(j), :] if first else outc.at[j]
        return remote(src, carry.at[j], cs_sem.at[j], cr_sem.at[j], tm + 2, co)

    def carry_back(j):
        return remote(carry.at[j], carry.at[j], cf_sem.at[j], cr_sem.at[j], tm - 1, co)

    @pl.when(first_chip)
    def _():
        row = lax.broadcasted_iota(jnp.int32, (rows, n), 0)
        col = lax.broadcasted_iota(jnp.int32, (rows, n), 1)
        pl.when(core == 1)(lambda: [carry_on(j, True).start() for j in range(nz)] and None)
        for j in range(nz):
            unit = jnp.where(row + chunk(j) * rows == col, F32(1.0), F32(0.0))
            for g in range(2):
                carry[j, g] = unit

    @pl.when(jnp.logical_not(first_chip) & jnp.logical_not(last_chip) & (core == 1))
    def _():
        for j in range(nz):
            carry_on(j, False).wait_recv()
            carry_back(j).start()
            for g in range(2):
                v = carry[j, g]
                hi = v.astype(BF16)
                outc[j, g] = times(jnp.stack([hi, (v - hi.astype(F32)).astype(BF16)]), qb[g])
            carry_on(j, False).start()

    sides = (z_up, z_down)

    def near(d, s):
        return order.index(half - s if d == 0 or s == 0 else s - half)

    def span(d, s):
        return (2 * d, 2) if s == 0 else (0, 4)

    def a_copy(d, s):
        m, c = span(d, s)
        src = wa.at[near(d, 0), pl.ds(m, c)] if s == 0 else ra.at[d, s - 1]
        return remote(src, ra.at[d, s, pl.ds(m, c)], as_sem.at[d, s], ar_sem.at[d, s], tm, sides[d])

    def a_step(d, s):
        j = near(d, s)
        if s > 0:
            a_copy(d, s - 1).wait_recv()
            m, c = span(d, s - 1)
            if c == 4:
                ra[d, s - 1] += wa[j]
            else:
                o = 2 - m
                ra[d, s - 1, m : m + 2] += wa[j, m : m + 2]
                ra[d, s - 1, o : o + 2] = wa[j, o : o + 2]
        a_copy(d, s).start()

    def yb_copy(j, o):
        src = wb.at[j, :, pl.ds(pl.multiple_of(y_peer(o) * sub, sub), sub), :]
        return remote(
            src, ryb.at[j, o - 1], ybs_sem.at[j, o - 1], ybr_sem.at[j, o - 1], tm, z * ny + y_peer(o)
        )

    summed = set()

    def yb_sum(j):
        if j not in summed:
            summed.add(j)
            for o in range(1, ny):
                yb_copy(j, o).wait_recv()
            v = wb[j, :, pl.ds(pl.multiple_of(y * sub, sub), sub), :]
            for o in range(1, ny):
                v = v + ryb[j, o - 1]
            rb[0, half + 1 + j] = v
        return rb[0, half + 1 + j]

    def b_copy(d, s):
        m, c = span(d, s)
        return remote(
            rb.at[d, s, pl.ds(m, c)], rb.at[d, s + 1, pl.ds(m, c)], bzs_sem.at[d, s], bzr_sem.at[d, s], tm, sides[d]
        )

    def b_step(d, s):
        v = yb_sum(near(d, s))
        if s > 0:
            b_copy(d, s - 1).wait_recv()
            m, c = span(d, s - 1)
            if c == 4:
                rb[d, s] += v
            else:
                o = 2 - m
                rb[d, s, m : m + 2] += v[m : m + 2]
                rb[d, s, o : o + 2] = v[o : o + 2]
        else:
            m, c = span(d, 0)
            rb[d, 0, m : m + c] = v[m : m + c]
        b_copy(d, s).start()

    blocks = chunk_blocks(nz)
    for k, block in enumerate(blocks):
        first, size = block[0], len(block)
        r = size * rows
        for j in block:
            @pl.when(jnp.logical_not(first_chip) & last_chip & (core == 1))
            def _():
                carry_on(j, False).wait_recv()
                carry_back(j).start()

            @pl.when(jnp.logical_not(first_chip) & (core == 0))
            def _():
                carry_back(j).wait_recv()

        def enter(g, _):
            v = carry[first : first + size, g].reshape(r, n)
            hi = v.astype(BF16)
            h = times(jnp.stack([hi, (v - hi.astype(F32)).astype(BF16)]), late[g])
            hi = h.astype(BF16)
            cab[g, 0, :r] = hi
            cab[g, 1, :r] = (h - hi.astype(F32)).astype(BF16)
            return 0

        lax.fori_loop(0, 2, enter, 0)

        def month(t, dst, m):
            total = None
            for g in range(2):
                v = times(cab[g, :, :r], pre[t, g])
                for i, j in enumerate(block):
                    cum_out[t, g, chunk_rows(j), :] = v[i * rows : (i + 1) * rows]
                w = share[g] * v
                total = w if total is None else total + w
            for i, j in enumerate(block):
                dst[j, m] = total[i * rows : (i + 1) * rows]

        def b_month(m, _):
            month(m + 4, wb, m)
            return 0

        def a_month(m, _):
            month(m, wa, m)
            return 0

        lax.fori_loop(0, 4, b_month, 0)
        for j in block:
            for o in range(1, ny):
                yb_copy(j, o).start()
        lax.fori_loop(0, 4, a_month, 0)
        for d in range(2):
            a_step(d, k)
        if k > 0:
            for d in range(2):
                b_step(d, k - 1)

    for s in range(len(blocks), half):
        for d in range(2):
            a_step(d, s)
        for d in range(2):
            b_step(d, s - 1)

    own_at = nz - 1
    v = wa[own_at]
    for d in range(2):
        a_copy(d, half - 1).wait_recv()
        v = v + ra[d, half - 1]
    wa[own_at] = v

    def ya_copy(o):
        src = wa.at[own_at, :, pl.ds(pl.multiple_of(y_peer(o) * sub, sub), sub), :]
        return remote(src, rya.at[o - 1], yas_sem.at[o - 1], yar_sem.at[o - 1], tm, z * ny + y_peer(o))

    for o in range(1, ny):
        ya_copy(o).start()
    for d in range(2):
        b_step(d, half - 1)
    v = yb_sum(own_at)
    for d in range(2):
        b_copy(d, half - 1).wait_recv()
        v = v + rb[d, half]
    pooled[4:8] = v
    v = wa[own_at, :, pl.ds(pl.multiple_of(y * sub, sub), sub), :]
    for o in range(1, ny):
        ya_copy(o).wait_recv()
        v = v + rya[o - 1]
    pooled[0:4] = v

    for i in range(3):
        pl.when(has_next)(lambda: fwd_halo(i).wait_send())
        pl.when(has_prev)(lambda: bwd_halo(i).wait_send())
    pl.when(core == 0)(lambda: send_t0().wait_send())
    for j in range(nz):
        pl.when((core == 1) & jnp.logical_not(last_chip))(lambda: carry_on(j, False).wait_send())
        pl.when((core == 1) & jnp.logical_not(first_chip))(lambda: carry_back(j).wait_send())
        for o in range(1, ny):
            yb_copy(j, o).wait_send()
    for d in range(2):
        for s in range(half):
            a_copy(d, s).wait_send()
            b_copy(d, s).wait_send()
    for o in range(1, ny):
        ya_copy(o).wait_send()


def on_device(nz, ny, transition, entry, share):
    n = transition.shape[-1]
    half, rows = nz // 2, n // nz
    sub = rows // ny
    widest = max(len(b) for b in chunk_blocks(nz))
    dma = pltpu.SemaphoreType.DMA
    return pl.pallas_call(
        functools.partial(kernel, nz, ny),
        out_shape=(
            OUT(transition.shape, F32),
            OUT((8, sub, n), F32),
        ),
        in_specs=[
            pl.BlockSpec(memory_space=pl.ANY),
            pl.BlockSpec(memory_space=pltpu.SMEM),
            pl.BlockSpec(memory_space=pltpu.SMEM),
        ],
        out_specs=(pl.BlockSpec(memory_space=pltpu.VMEM), pl.BlockSpec(memory_space=pltpu.VMEM)),
        scratch_shapes=[
            pltpu.VMEM((8, 2, n, n), F32),
            pltpu.VMEM((3, 2, n, n), F32),
            pltpu.VMEM((3, 2, n, n), F32),
            pltpu.VMEM((8, 2, 2, n, n), BF16),
            pltpu.VMEM((8, 2, 2, n, n), BF16),
            pltpu.VMEM((2, n, n), F32),
            pltpu.VMEM((2, n, n), F32),
            pltpu.VMEM((2, 2, n, n), BF16),
            pltpu.VMEM((2, n, n), F32),
            pltpu.VMEM((2, 2, n, n), BF16),
            pltpu.VMEM((nz, 2, rows, n), F32),
            pltpu.VMEM((nz, 2, rows, n), F32),
            pltpu.VMEM((2, 2, widest * rows, n), BF16),
            pltpu.VMEM((nz, 4, rows, n), F32),
            pltpu.VMEM((nz, 4, rows, n), F32),
            pltpu.VMEM((2, half, 4, rows, n), F32),
            pltpu.VMEM((2, half + 1 + nz, 4, sub, n), F32),
            pltpu.VMEM((ny - 1, 4, sub, n), F32),
            pltpu.VMEM((nz, ny - 1, 4, sub, n), F32),
            dma((8,)), dma((3,)), dma((3,)), dma((3,)), dma((3,)), dma((2,)),
            dma((nz,)), dma((nz,)), dma((nz,)),
            dma((2, half)), dma((2, half)), dma((2, half)), dma((2, half)),
            dma((ny - 1,)), dma((ny - 1,)), dma((nz, ny - 1)), dma((nz, ny - 1)),
        ],
        compiler_params=pltpu.CompilerParams(
            collective_id=0, has_side_effects=True, vmem_limit_bytes=VMEM_LIMIT
        ),
        cost_estimate=pl.CostEstimate(
            flops=3 * 2 * 46 * n**3, bytes_accessed=2 * 4 * 16 * n * n, transcendentals=0
        ),
    )(transition, entry, share)


def solution(mesh, nz=8, ny=4):
    return jax.shard_map(
        functools.partial(on_device, nz, ny),
        mesh=mesh,
        in_specs=(P("tm", "cohort", None, None), P("cohort"), P("cohort")),
        out_specs=(P("tm", "cohort", None, None), P("tm", "cohort", None)),
        check_vma=False,
    )
```

```python
import functools

import jax
import jax.numpy as jnp
from jax import lax
from jax.experimental import pallas as pl
from jax.experimental.pallas import tpu as pltpu
from jax.sharding import PartitionSpec as P

MESH = pl.DeviceIdType.MESH
F32 = jnp.float32
BF16 = jnp.bfloat16
OUT = pltpu.VMEM
VMEM_LIMIT = 48 * 1024 * 1024


def chunk_blocks(nz):
    half = nz // 2
    blocks = [[d, -d] for d in range(half - 1, 0, -1)]
    blocks[0].insert(0, half)
    blocks[-1].append(0)
    return blocks


def kernel(
    nz, ny, trans, entry_in, share_in, cum_out, pooled, entry, share,
    own, hp, hn, mon, pre, t0s, t0r, late, qs, qb, carry, outc, cab, wa, wb, ra, fa, rb, fb, rya, ryb, ysum,
    in_sem, own_sem, fs_sem, bs_sem, hp_sem, hn_sem, t0_sem, cs_sem, cr_sem, cf_sem,
    as_sem, ar_sem, fas_sem, far_sem, bzs_sem, bzr_sem, fbs_sem, fbr_sem, yas_sem, yar_sem, ybs_sem, ybr_sem,
):
    n = own.shape[-1]
    half = nz // 2
    rows = n // nz
    sub = rows // ny
    blocks = chunk_blocks(nz)
    order = sum(blocks, [])
    tm = lax.axis_index("tm")
    co = lax.axis_index("cohort")
    ntm = lax.axis_size("tm")
    core, chip = lax.rem(tm, 2), tm // 2
    z, y = co // ny, lax.rem(co, ny)
    has_prev, has_next = tm > 0, tm < ntm - 1
    first_chip, last_chip = chip == 0, chip == ntm // 2 - 1

    def z_at(k):
        return lax.rem(z + nz + k, nz) * ny + y

    def y_peer(o):
        return lax.rem(y + o, ny)

    small = [pltpu.make_async_copy(entry_in, entry, in_sem.at[0]), pltpu.make_async_copy(share_in, share, in_sem.at[1])]
    for copy in small:
        copy.start()

    barrier = pltpu.get_barrier_semaphore()

    def greet(t, c):
        pl.semaphore_signal(barrier, inc=1, device_id=(t, c), device_id_type=MESH)

    near = (
        (has_prev, tm - 1), (has_next, tm + 1),
        ((core == 1) & (tm > 1), tm - 2), ((core == 1) & (tm < ntm - 2), tm + 2),
    )
    peers = 3 + ny
    for cond, t in near:
        pl.when(cond)(functools.partial(greet, t, co))
        peers = peers + jnp.where(cond, 1, 0)
    for c in [z_at(k) for k in (1, -1, 2, -2)] + [z * ny + y_peer(o) for o in range(1, ny)]:
        greet(tm, c)
    pl.semaphore_wait(barrier, peers)

    def remote(src, dst, ss, rs, t, c):
        return pltpu.make_async_remote_copy(
            src_ref=src, dst_ref=dst, send_sem=ss, recv_sem=rs, device_id=(t, c), device_id_type=MESH
        )

    def fwd_halo(i):
        return remote(trans.at[5 + i], hp.at[i], fs_sem.at[i], hp_sem.at[i], tm + 1, co)

    def bwd_halo(i):
        return remote(trans.at[i], hn.at[i], bs_sem.at[i], hn_sem.at[i], tm - 1, co)

    def own_copy(i):
        return pltpu.make_async_copy(trans.at[i], own.at[i], own_sem.at[i])

    def send_fwd():
        for i in (2, 1, 0):
            fwd_halo(i).start()

    def send_bwd():
        for i in (0, 1, 2):
            bwd_halo(i).start()

    pl.when((core == 0) & has_prev)(send_bwd)
    pl.when(has_next)(send_fwd)
    pl.when((core == 1) & has_prev)(send_bwd)

    for i in range(8):
        own_copy(i).start()

    @pl.when(jnp.logical_not(has_prev))
    def _():
        hp[...] = jnp.zeros_like(hp)

    @pl.when(jnp.logical_not(has_next))
    def _():
        hn[...] = jnp.zeros_like(hn)

    strip = min(64, n)

    def graduate(t):
        def at(e):
            return (hp, e + 3) if e < 0 else ((hn, e - 8) if e > 7 else (own, e))

        edge = {0: 10, 1: 13, 2: 15, 5: 15, 6: 13, 7: 10}.get(t)
        scale = 1.0 / 16
        if edge is not None:
            scale = jnp.where(tm == (0 if t < 3 else ntm - 1), F32(1.0 / edge), F32(1.0 / 16))

        def step(i, _):
            g, r0 = i // (n // strip), pl.multiple_of(lax.rem(i, n // strip) * strip, strip)
            act = jnp.where(8 * tm + t >= entry[g], F32(1.0), F32(0.0))

            def load(e):
                ref, k = at(e)
                return ref[k, g, pl.ds(r0, strip), :]

            total = (
                4.0 * load(t) + 3.0 * (load(t - 1) + load(t + 1))
                + 2.0 * (load(t - 2) + load(t + 2)) + (load(t - 3) + load(t + 3))
            )
            row = lax.broadcasted_iota(jnp.int32, (strip, n), 0) + r0
            col = lax.broadcasted_iota(jnp.int32, (strip, n), 1)
            unit = jnp.where(row == col, 1.0 - act, 0.0)
            v = total * (act * scale) + unit
            hi = v.astype(BF16)
            mon[t, g, 0, pl.ds(r0, strip), :] = hi
            mon[t, g, 1, pl.ds(r0, strip), :] = (v - hi.astype(F32)).astype(BF16)
            return 0

        lax.fori_loop(0, 2 * (n // strip), step, 0)

    def dot(a, b):
        return jnp.dot(a, b, preferred_element_type=F32)

    def times(a, b):
        r = a.shape[1]
        both = dot(a.reshape(2 * r, n), b[0])
        return both[:r] + both[r:] + dot(a[0], b[1])

    def halves(ref, v):
        hi = v.astype(BF16)
        ref[0] = hi
        ref[1] = (v - hi.astype(F32)).astype(BF16)

    def multiply(dst, a, b, keep=None):
        def step(g, _):
            v = times(a(g), b(g))
            halves(dst.at[g], v)
            if keep is not None:
                keep[g] = v
            return 0
        lax.fori_loop(0, 2, step, 0)

    def take(ref, k):
        return lambda g: ref[k, g]

    def copy_pre(t):
        pre[t] = mon[t]

    def fwd_wait(i):
        pl.when(has_prev)(lambda: fwd_halo(i).wait_recv())

    def bwd_wait(i):
        pl.when(has_next)(lambda: bwd_halo(i).wait_recv())

    for copy in small:
        copy.wait()
    for i in range(8):
        own_copy(i).wait()
    graduate(3)
    graduate(4)

    def send_t0():
        return remote(t0s, t0r, t0_sem.at[0], t0_sem.at[1], tm + 1, co)

    @pl.when(core == 0)
    def _():
        for i in range(3):
            bwd_wait(i)
            graduate(5 + i)
        copy_pre(3)
        for t in range(4, 8):
            multiply(pre.at[t], take(pre, t - 1), take(mon, t))
        fwd_wait(2)
        graduate(2)
        fwd_wait(1)
        graduate(1)
        copy_pre(1)
        multiply(pre.at[2], take(mon, 1), take(mon, 2))
        for t in range(3, 8):
            multiply(pre.at[t], take(pre, 2), take(pre, t))
        row = lax.broadcasted_iota(jnp.int32, (n, n), 0)
        col = lax.broadcasted_iota(jnp.int32, (n, n), 1)
        for g in range(2):
            halves(pre.at[0, g], jnp.where(row == col, F32(1.0), F32(0.0)))
        fwd_wait(0)
        graduate(0)
        multiply(qb, take(mon, 0), take(pre, 7), t0s)
        send_t0().start()
        late[...] = mon[0]

    @pl.when(core == 1)
    def _():
        for i in (2, 1, 0):
            fwd_wait(i)
            graduate(i)
        copy_pre(0)
        for t in range(1, 5):
            multiply(pre.at[t], take(pre, t - 1), take(mon, t))
        for t in range(5, 8):
            bwd_wait(t - 5)
            graduate(t)
            multiply(pre.at[t], take(pre, t - 1), take(mon, t))
        send_t0().wait_recv()
        for g in range(2):
            halves(late.at[g], t0r[g])
        pl.when(jnp.logical_not(last_chip))(
            lambda: multiply(qb, lambda g: late[g], take(pre, 7), qs)
        )

    def chunk(j):
        return lax.rem(z + nz + order[j], nz)

    def chunk_rows(j):
        return pl.ds(pl.multiple_of(chunk(j) * rows, rows), rows)

    def carry_on(j, g, first=False):
        src = qs.at[g, chunk_rows(j), :] if first else outc.at[j, g]
        return remote(src, carry.at[j, g], cs_sem.at[j, g], cr_sem.at[j, g], tm + 2, co)

    def carry_back(j, g):
        return remote(carry.at[j, g], carry.at[j, g], cf_sem.at[j, g], cr_sem.at[j, g], tm - 1, co)

    pieces = [(j, g) for j in range(nz) for g in range(2)]

    @pl.when(first_chip)
    def _():
        row = lax.broadcasted_iota(jnp.int32, (rows, n), 0)
        col = lax.broadcasted_iota(jnp.int32, (rows, n), 1)
        pl.when(core == 1)(lambda: [carry_on(j, g, True).start() for j, g in pieces] and None)
        for j in range(nz):
            unit = jnp.where(row + chunk(j) * rows == col, F32(1.0), F32(0.0))
            for g in range(2):
                carry[j, g] = unit

    middle = jnp.logical_not(first_chip) & jnp.logical_not(last_chip) & (core == 1)

    def hand_on(some):
        for j, g in some:
            carry_on(j, g).wait_recv()
            v = carry[j, g]
            hi = v.astype(BF16)
            outc[j, g] = times(jnp.stack([hi, (v - hi.astype(F32)).astype(BF16)]), qb[g])
            carry_on(j, g).start()
            carry_back(j, g).start()

    ahead = min(2 * nz, 2 * len(blocks[0]) + 4)
    pl.when(middle)(lambda: hand_on(pieces[:ahead]))

    def place(d, s):
        return order.index(half - s if d == 0 else s - half)

    def z_side(d, k=1):
        return z_at(k if d == 0 else -k)

    def a_copy(d, s, m):
        src = wa.at[place(d, 1), m] if s == 1 else ra.at[d, s - 2, m]
        return remote(src, ra.at[d, s - 1, m], as_sem.at[d, s - 1, m], ar_sem.at[d, s - 1, m], tm, z_side(d))

    def a_far(d, i):
        return remote(wa.at[0, 2 * d + i], fa.at[d, i], fas_sem.at[d, i], far_sem.at[d, i], tm, z_side(d, 2))

    def a_come(d, s, m):
        parts = []
        if s >= 2:
            a_copy(d, s - 1, m).wait_recv()
            parts.append(ra[d, s - 2, m])
        if s == 2 and m // 2 == d:
            a_far(d, m % 2).wait_recv()
            parts.append(fa[d, m % 2])
        return parts

    def a_stage(s, months=range(4)):
        for m in months:
            for d in range(2):
                ra[d, s - 2, m] = sum(a_come(d, s, m), wa[place(d, s), m])
                a_copy(d, s, m).start()

    def yb_copy(j, h, o):
        rows_to = pl.ds(pl.multiple_of(y_peer(o) * sub, sub), sub)
        return remote(
            wb.at[j, pl.ds(2 * h, 2), rows_to, :], ryb.at[j, o - 1, pl.ds(2 * h, 2)],
            ybs_sem.at[j, h, o - 1], ybr_sem.at[j, h, o - 1], tm, z * ny + y_peer(o),
        )

    summed = set()

    def yb_sum(j):
        if j not in summed:
            summed.add(j)
            v = wb[j, :, pl.ds(pl.multiple_of(y * sub, sub), sub), :]
            for o in range(1, ny):
                for h in range(2):
                    yb_copy(j, h, o).wait_recv()
                v = v + ryb[j, o - 1]
            ysum[j] = v

    def b_copy(d, s):
        return remote(rb.at[d, s - 1], rb.at[d, s], bzs_sem.at[d, s - 1], bzr_sem.at[d, s - 1], tm, z_side(d))

    def b_far(d):
        return remote(
            ysum.at[0, pl.ds(2 * d, 2)], fb.at[d], fbs_sem.at[d], fbr_sem.at[d], tm, z_side(d, 2)
        )

    def b_stage(s):
        if s == 1:
            yb_sum(0)
            for d in range(2):
                b_far(d).start()
        for d in range(2):
            j = place(d, s)
            yb_sum(j)
            if s == 1:
                rb[d, 0] = ysum[j]
            else:
                b_copy(d, s - 1).wait_recv()
                rb[d, s - 1] += ysum[j]
            if s == 2:
                b_far(d).wait_recv()
                rb[d, 1, 2 * d : 2 * d + 2] += fb[d]
            b_copy(d, s).start()

    first = 0
    for k in range(len(blocks)):
        size = len(blocks[k])
        block = range(first, first + size)
        r = size * rows
        for j in block:
            @pl.when(jnp.logical_not(first_chip) & last_chip & (core == 1))
            def _():
                for g in range(2):
                    carry_on(j, g).wait_recv()
                    carry_back(j, g).start()

            @pl.when(jnp.logical_not(first_chip) & (core == 0))
            def _():
                for g in range(2):
                    carry_back(j, g).wait_recv()

        def enter(g, _):
            v = carry[first : first + size, g].reshape(r, n)
            hi = v.astype(BF16)
            h = times(jnp.stack([hi, (v - hi.astype(F32)).astype(BF16)]), late[g])
            hi = h.astype(BF16)
            cab[g, 0, :r] = hi
            cab[g, 1, :r] = (h - hi.astype(F32)).astype(BF16)
            return 0

        lax.fori_loop(0, 2, enter, 0)

        def month(t, dst, m):
            total = None
            for g in range(2):
                v = times(cab[g, :, :r], pre[t, g])
                for i, j in enumerate(block):
                    cum_out[t, g, chunk_rows(j), :] = v[i * rows : (i + 1) * rows]
                w = share[g] * v
                total = w if total is None else total + w
            for i, j in enumerate(block):
                dst[j, m] = total[i * rows : (i + 1) * rows]

        def b_month(m, _):
            month(m + 4, wb, m)
            return 0

        def a_month(m, _):
            month(m, wa, m)
            return 0

        for h in range(2):
            if k == 0:
                for m in (2 * h, 2 * h + 1):
                    month(m, wa, m)
                    for d in range(2):
                        a_copy(d, 1, m).start()
                    a_far(h, m % 2).start()
            else:
                lax.fori_loop(2 * h, 2 * h + 2, a_month, 0)
            lax.fori_loop(2 * h, 2 * h + 2, b_month, 0)
            for j in block:
                for o in range(1, ny):
                    yb_copy(j, h, o).start()
            if k == len(blocks) - 1 and half > 2:
                a_stage(2, (2 * h, 2 * h + 1))
        if k == 0 and ahead < 2 * nz:
            pl.when(middle)(lambda: hand_on(pieces[ahead:]))
        first += size

    for s in range(1, half - 1):
        if s > 1:
            a_stage(s + 1)
        b_stage(s)

    own_at = nz - 1
    for m in range(4):
        v = wa[own_at, m]
        for d in range(2):
            v = sum(a_come(d, half, m), v)
        wa[own_at, m] = v

    def ya_copy(o):
        src = wa.at[own_at, :, pl.ds(pl.multiple_of(y_peer(o) * sub, sub), sub), :]
        return remote(src, rya.at[o - 1], yas_sem.at[o - 1], yar_sem.at[o - 1], tm, z * ny + y_peer(o))

    for o in range(1, ny):
        ya_copy(o).start()
    b_stage(half - 1)
    for i in range(3):
        pl.when(has_next)(lambda: fwd_halo(i).wait_send())
        pl.when(has_prev)(lambda: bwd_halo(i).wait_send())
    pl.when(core == 0)(lambda: send_t0().wait_send())
    for j in range(nz):
        for g in range(2):
            pl.when((core == 1) & jnp.logical_not(last_chip))(lambda: carry_on(j, g).wait_send())
            pl.when((core == 1) & jnp.logical_not(first_chip))(lambda: carry_back(j, g).wait_send())
        for o in range(1, ny):
            for h in range(2):
                yb_copy(j, h, o).wait_send()
    for d in range(2):
        b_far(d).wait_send()
        for i in range(2):
            a_far(d, i).wait_send()
        for s in range(1, half):
            b_copy(d, s).wait_send()
            for m in range(4):
                a_copy(d, s, m).wait_send()

    yb_sum(own_at)
    v = ysum[own_at]
    for d in range(2):
        b_copy(d, half - 1).wait_recv()
        v = v + rb[d, half - 1]
    pooled[4:8] = v
    if half == 2:
        for d in range(2):
            b_far(d).wait_recv()
            pooled[4 + 2 * d : 6 + 2 * d] += fb[d]
    v = wa[own_at, :, pl.ds(pl.multiple_of(y * sub, sub), sub), :]
    for o in range(1, ny):
        ya_copy(o).wait_recv()
        v = v + rya[o - 1]
    pooled[0:4] = v
    for o in range(1, ny):
        ya_copy(o).wait_send()


def deliver(cum, pooled, cum_out, pooled_out, sem):
    copies = [pltpu.make_async_copy(pooled, pooled_out, sem.at[8])]
    for i in range(8):
        part = pl.ds(i, 1)
        copies.append(pltpu.make_async_copy(cum.at[part], cum_out.at[part], sem.at[i]))
    for copy in copies:
        copy.start()
    for copy in copies:
        copy.wait()


def on_device(nz, ny, transition, entry, share):
    n = transition.shape[-1]
    half, rows = nz // 2, n // nz
    sub = rows // ny
    widest = max(len(b) for b in chunk_blocks(nz))
    dma = pltpu.SemaphoreType.DMA
    cum, pooled = pl.pallas_call(
        functools.partial(kernel, nz, ny),
        out_shape=(
            OUT(transition.shape, F32),
            OUT((8, sub, n), F32),
        ),
        in_specs=[
            pl.BlockSpec(memory_space=pltpu.HBM),
            pl.BlockSpec(memory_space=pltpu.HBM),
            pl.BlockSpec(memory_space=pltpu.HBM),
        ],
        out_specs=(pl.BlockSpec(memory_space=pltpu.VMEM), pl.BlockSpec(memory_space=pltpu.VMEM)),
        scratch_shapes=[
            pltpu.SMEM(entry.shape, entry.dtype),
            pltpu.SMEM(share.shape, F32),
            pltpu.VMEM((8, 2, n, n), F32),
            pltpu.VMEM((3, 2, n, n), F32),
            pltpu.VMEM((3, 2, n, n), F32),
            pltpu.VMEM((8, 2, 2, n, n), BF16),
            pltpu.VMEM((8, 2, 2, n, n), BF16),
            pltpu.VMEM((2, n, n), F32),
            pltpu.VMEM((2, n, n), F32),
            pltpu.VMEM((2, 2, n, n), BF16),
            pltpu.VMEM((2, n, n), F32),
            pltpu.VMEM((2, 2, n, n), BF16),
            pltpu.VMEM((nz, 2, rows, n), F32),
            pltpu.VMEM((nz, 2, rows, n), F32),
            pltpu.VMEM((2, 2, widest * rows, n), BF16),
            pltpu.VMEM((nz, 4, rows, n), F32),
            pltpu.VMEM((nz, 4, rows, n), F32),
            pltpu.VMEM((2, half - 1, 4, rows, n), F32),
            pltpu.VMEM((2, 2, rows, n), F32),
            pltpu.VMEM((2, half, 4, sub, n), F32),
            pltpu.VMEM((2, 2, sub, n), F32),
            pltpu.VMEM((ny - 1, 4, sub, n), F32),
            pltpu.VMEM((nz, ny - 1, 4, sub, n), F32),
            pltpu.VMEM((nz, 4, sub, n), F32),
            dma((2,)), dma((8,)), dma((3,)), dma((3,)), dma((3,)), dma((3,)), dma((2,)),
            dma((nz, 2)), dma((nz, 2)), dma((nz, 2)),
            dma((2, half - 1, 4)), dma((2, half - 1, 4)), dma((2, 2)), dma((2, 2)),
            dma((2, half - 1)), dma((2, half - 1)), dma((2,)), dma((2,)),
            dma((ny - 1,)), dma((ny - 1,)), dma((nz, 2, ny - 1)), dma((nz, 2, ny - 1)),
        ],
        compiler_params=pltpu.CompilerParams(
            collective_id=0, has_side_effects=True, vmem_limit_bytes=VMEM_LIMIT
        ),
        cost_estimate=pl.CostEstimate(
            flops=3 * 2 * 46 * n**3, bytes_accessed=2 * 4 * 16 * n * n, transcendentals=0
        ),
    )(transition, *(pltpu.with_memory_space_constraint(a, pltpu.HBM) for a in (entry, share)))
    return pl.pallas_call(
        deliver,
        out_shape=(jax.ShapeDtypeStruct(cum.shape, F32), jax.ShapeDtypeStruct(pooled.shape, F32)),
        in_specs=[pl.BlockSpec(memory_space=pltpu.VMEM)] * 2,
        out_specs=[pl.BlockSpec(memory_space=pl.ANY)] * 2,
        scratch_shapes=[dma((9,))],
        compiler_params=pltpu.CompilerParams(vmem_limit_bytes=1024 * 1024),
    )(*(pltpu.with_memory_space_constraint(a, pltpu.VMEM) for a in (cum, pooled)))


def solution(mesh, nz=8, ny=4):
    return jax.shard_map(
        functools.partial(on_device, nz, ny),
        mesh=mesh,
        in_specs=(P("tm", "cohort", None, None), P("cohort"), P("cohort")),
        out_specs=(P("tm", "cohort", None, None), P("tm", "cohort", None)),
        check_vma=False,
    )
```

```python
import functools

import jax
import jax.numpy as jnp
from jax import lax
from jax.experimental import pallas as pl
from jax.experimental.pallas import tpu as pltpu
from jax.sharding import PartitionSpec as P

MESH = pl.DeviceIdType.MESH
F32 = jnp.float32
BF16 = jnp.bfloat16
OUT = pltpu.VMEM
VMEM_LIMIT = 48 * 1024 * 1024


def chunk_blocks(nz):
    half = nz // 2
    blocks = [[d, -d] for d in range(half - 1, 0, -1)]
    blocks[0].insert(0, half)
    blocks[-1].append(0)
    return blocks


def kernel(
    nz, ny, trans, entry_in, share_in, cum_out, pooled, entry, share,
    own, hp, hn, mon, pre, t0s, t0r, late, qs, qb, carry, outc, cab, wa, wb, ra, fa, rb, fb, rya, ryb, ysum,
    in_sem, own_sem, fs_sem, bs_sem, hp_sem, hn_sem, t0_sem, cs_sem, cr_sem, cf_sem,
    as_sem, ar_sem, fas_sem, far_sem, bzs_sem, bzr_sem, fbs_sem, fbr_sem, yas_sem, yar_sem, ybs_sem, ybr_sem,
):
    n = own.shape[-1]
    half = nz // 2
    rows = n // nz
    sub = rows // ny
    blocks = chunk_blocks(nz)
    order = sum(blocks, [])
    tm = lax.axis_index("tm")
    co = lax.axis_index("cohort")
    ntm = lax.axis_size("tm")
    core, chip = lax.rem(tm, 2), tm // 2
    z, y = co // ny, lax.rem(co, ny)
    has_prev, has_next = tm > 0, tm < ntm - 1
    first_chip, last_chip = chip == 0, chip == ntm // 2 - 1

    def z_at(k):
        return lax.rem(z + nz + k, nz) * ny + y

    def y_peer(o):
        return lax.rem(y + o, ny)

    small = [pltpu.make_async_copy(entry_in, entry, in_sem.at[0]), pltpu.make_async_copy(share_in, share, in_sem.at[1])]
    for copy in small:
        copy.start()

    barrier = pltpu.get_barrier_semaphore()

    def greet(t, c):
        pl.semaphore_signal(barrier, inc=1, device_id=(t, c), device_id_type=MESH)

    near = (
        (has_prev, tm - 1), (has_next, tm + 1),
        ((core == 1) & (tm > 1), tm - 2), ((core == 1) & (tm < ntm - 2), tm + 2),
    )
    peers = 3 + ny
    for cond, t in near:
        pl.when(cond)(functools.partial(greet, t, co))
        peers = peers + jnp.where(cond, 1, 0)
    for c in [z_at(k) for k in (1, -1, 2, -2)] + [z * ny + y_peer(o) for o in range(1, ny)]:
        greet(tm, c)
    pl.semaphore_wait(barrier, peers)

    def remote(src, dst, ss, rs, t, c):
        return pltpu.make_async_remote_copy(
            src_ref=src, dst_ref=dst, send_sem=ss, recv_sem=rs, device_id=(t, c), device_id_type=MESH
        )

    def fwd_halo(i):
        return remote(trans.at[5 + i], hp.at[i], fs_sem.at[i], hp_sem.at[i], tm + 1, co)

    def bwd_halo(i):
        return remote(trans.at[i], hn.at[i], bs_sem.at[i], hn_sem.at[i], tm - 1, co)

    def own_copy(i):
        return pltpu.make_async_copy(trans.at[i], own.at[i], own_sem.at[i])

    def send_fwd():
        for i in (2, 1, 0):
            fwd_halo(i).start()

    def send_bwd():
        for i in (0, 1, 2):
            bwd_halo(i).start()

    pl.when((core == 0) & has_prev)(send_bwd)
    pl.when(has_next)(send_fwd)
    pl.when((core == 1) & has_prev)(send_bwd)

    for i in range(8):
        own_copy(i).start()

    @pl.when(jnp.logical_not(has_prev))
    def _():
        hp[...] = jnp.zeros_like(hp)

    @pl.when(jnp.logical_not(has_next))
    def _():
        hn[...] = jnp.zeros_like(hn)

    strip = min(64, n)

    def graduate(t, part=None, groups=None):
        def at(e):
            return (hp, e + 3) if e < 0 else ((hn, e - 8) if e > 7 else (own, e))

        edge = {0: 10, 1: 13, 2: 15, 5: 15, 6: 13, 7: 10}.get(t)
        scale = 1.0 / 16
        if edge is not None:
            scale = jnp.where(tm == (0 if t < 3 else ntm - 1), F32(1.0 / edge), F32(1.0 / 16))
        last, other = (t - 3, t + 3) if t == 0 else (t + 3, t - 3)
        strips = n // strip
        low = 0 if groups is None else groups[0] * strips
        high = 2 * strips if groups is None else (groups[-1] + 1) * strips

        def step(i, _):
            g, r0 = i // strips, pl.multiple_of(lax.rem(i, strips) * strip, strip)
            here = pl.ds(r0, strip)

            def load(e):
                ref, k = at(e)
                return ref[k, g, here, :]

            if groups is None:
                total = (
                    4.0 * load(t) + 3.0 * (load(t - 1) + load(t + 1))
                    + 2.0 * (load(t - 2) + load(t + 2)) + load(other)
                )
                if part is not None:
                    part[g, here, :] = total
                    return 0
            else:
                total = part[g, here, :]
            act = jnp.where(8 * tm + t >= entry[g], F32(1.0), F32(0.0))
            row = lax.broadcasted_iota(jnp.int32, (strip, n), 0) + r0
            col = lax.broadcasted_iota(jnp.int32, (strip, n), 1)
            unit = jnp.where(row == col, 1.0 - act, 0.0)
            v = (total + load(last)) * (act * scale) + unit
            hi = v.astype(BF16)
            mon[t, g, 0, here, :] = hi
            mon[t, g, 1, here, :] = (v - hi.astype(F32)).astype(BF16)
            return 0

        lax.fori_loop(low, high, step, 0)

    def dot(a, b):
        return jnp.dot(a, b, preferred_element_type=F32)

    def times(a, b):
        r = a.shape[1]
        both = dot(a.reshape(2 * r, n), b[0])
        return both[:r] + both[r:] + dot(a[0], b[1])

    def halves(ref, v):
        hi = v.astype(BF16)
        ref[0] = hi
        ref[1] = (v - hi.astype(F32)).astype(BF16)

    def multiply(dst, a, b, keep=None):
        def step(g, _):
            v = times(a(g), b(g))
            halves(dst.at[g], v)
            if keep is not None:
                keep[g] = v
            return 0
        lax.fori_loop(0, 2, step, 0)

    def take(ref, k):
        return lambda g: ref[k, g]

    def copy_pre(t):
        pre[t] = mon[t]

    def fwd_wait(i):
        pl.when(has_prev)(lambda: fwd_halo(i).wait_recv())

    def bwd_wait(i):
        pl.when(has_next)(lambda: bwd_halo(i).wait_recv())

    for copy in small:
        copy.wait()
    for i in range(8):
        own_copy(i).wait()
    graduate(3)
    graduate(4)

    def send_t0(g):
        return remote(t0s.at[g], t0r.at[g], t0_sem.at[0, g], t0_sem.at[1, g], tm + 1, co)

    def chunk(j):
        return lax.rem(z + nz + order[j], nz)

    def chunk_rows(j):
        return pl.ds(pl.multiple_of(chunk(j) * rows, rows), rows)

    def carry_on(j, g, first=False):
        src = qs.at[g, chunk_rows(j), :] if first else outc.at[j, g]
        return remote(src, carry.at[j, g], cs_sem.at[j, g], cr_sem.at[j, g], tm + 2, co)

    def carry_back(j, g):
        return remote(carry.at[j, g], carry.at[j, g], cf_sem.at[j, g], cr_sem.at[j, g], tm - 1, co)

    pieces = [(j, g) for j in range(nz) for g in range(2)]

    soon = len(blocks[0])

    def take_late(g):
        return late[g]

    @pl.when(core == 0)
    def _():
        for i in range(3):
            bwd_wait(i)
            graduate(5 + i)
        copy_pre(3)
        for t in range(4, 8):
            multiply(pre.at[t], take(pre, t - 1), take(mon, t))
        fwd_wait(2)
        graduate(2)
        fwd_wait(1)
        graduate(1)
        copy_pre(1)
        multiply(pre.at[2], take(mon, 1), take(mon, 2))
        for t in range(3, 8):
            multiply(pre.at[t], take(pre, 2), take(pre, t))
        row = lax.broadcasted_iota(jnp.int32, (n, n), 0)
        col = lax.broadcasted_iota(jnp.int32, (n, n), 1)
        for g in range(2):
            halves(pre.at[0, g], jnp.where(row == col, F32(1.0), F32(0.0)))
        graduate(0, qs)
        fwd_wait(0)
        for g in range(2):
            graduate(0, qs, [g])
            t0s[g] = times(mon[0, g], pre[7, g])
            send_t0(g).start()
        late[...] = mon[0]

    @pl.when(core == 1)
    def _():
        for i in (2, 1, 0):
            fwd_wait(i)
            graduate(i)
        copy_pre(0)
        for t in range(1, 5):
            multiply(pre.at[t], take(pre, t - 1), take(mon, t))
        for t in (5, 6):
            bwd_wait(t - 5)
            graduate(t)
            multiply(pre.at[t], take(pre, t - 1), take(mon, t))
        graduate(7, t0s)

        @pl.when(first_chip)
        def _():
            for g in range(2):
                send_t0(g).wait_recv()
                halves(late.at[g], t0r[g])
            multiply(qb, take_late, take(pre, 6))
            bwd_wait(2)
            for g in range(2):
                graduate(7, t0s, [g])
                qs[g] = times(qb[g], mon[7, g])
                for j in range(soon):
                    carry_on(j, g, True).start()
            for j in range(soon, nz):
                for g in range(2):
                    carry_on(j, g, True).start()
            multiply(pre.at[7], take(pre, 6), take(mon, 7))

        @pl.when(jnp.logical_not(first_chip))
        def _():
            bwd_wait(2)
            graduate(7, t0s, [0, 1])
            multiply(pre.at[7], take(pre, 6), take(mon, 7))
            for g in range(2):
                send_t0(g).wait_recv()
                halves(late.at[g], t0r[g])

                @pl.when(jnp.logical_not(last_chip))
                def _():
                    halves(qb.at[g], times(late[g], pre[7, g]))

    @pl.when(first_chip)
    def _():
        row = lax.broadcasted_iota(jnp.int32, (rows, n), 0)
        col = lax.broadcasted_iota(jnp.int32, (rows, n), 1)
        for j in range(nz):
            unit = jnp.where(row + chunk(j) * rows == col, F32(1.0), F32(0.0))
            for g in range(2):
                carry[j, g] = unit

    middle = jnp.logical_not(first_chip) & jnp.logical_not(last_chip) & (core == 1)

    def hand_on(some):
        for j, g in some:
            carry_on(j, g).wait_recv()
            v = carry[j, g]
            hi = v.astype(BF16)
            outc[j, g] = times(jnp.stack([hi, (v - hi.astype(F32)).astype(BF16)]), qb[g])
            carry_on(j, g).start()
            carry_back(j, g).start()

    ahead = min(2 * nz, 2 * len(blocks[0]) + 4)
    pl.when(middle)(lambda: hand_on(pieces[:ahead]))

    def place(d, s):
        return order.index(half - s if d == 0 else s - half)

    def z_side(d, k=1):
        return z_at(k if d == 0 else -k)

    def a_copy(d, s, m):
        src = wa.at[place(d, 1), m] if s == 1 else ra.at[d, s - 2, m]
        return remote(src, ra.at[d, s - 1, m], as_sem.at[d, s - 1, m], ar_sem.at[d, s - 1, m], tm, z_side(d))

    def a_far(d, i):
        return remote(wa.at[0, 2 * d + i], fa.at[d, i], fas_sem.at[d, i], far_sem.at[d, i], tm, z_side(d, 2))

    def a_come(d, s, m):
        parts = []
        if s >= 2:
            a_copy(d, s - 1, m).wait_recv()
            parts.append(ra[d, s - 2, m])
        if s == 2 and m // 2 == d:
            a_far(d, m % 2).wait_recv()
            parts.append(fa[d, m % 2])
        return parts

    def a_stage(s, months=range(4)):
        for m in months:
            for d in range(2):
                ra[d, s - 2, m] = sum(a_come(d, s, m), wa[place(d, s), m])
                a_copy(d, s, m).start()

    def yb_copy(j, h, o):
        rows_to = pl.ds(pl.multiple_of(y_peer(o) * sub, sub), sub)
        return remote(
            wb.at[j, pl.ds(2 * h, 2), rows_to, :], ryb.at[j, o - 1, pl.ds(2 * h, 2)],
            ybs_sem.at[j, h, o - 1], ybr_sem.at[j, h, o - 1], tm, z * ny + y_peer(o),
        )

    summed = set()

    def yb_sum(j):
        if j not in summed:
            summed.add(j)
            v = wb[j, :, pl.ds(pl.multiple_of(y * sub, sub), sub), :]
            for o in range(1, ny):
                for h in range(2):
                    yb_copy(j, h, o).wait_recv()
                v = v + ryb[j, o - 1]
            ysum[j] = v

    def b_copy(d, s):
        return remote(rb.at[d, s - 1], rb.at[d, s], bzs_sem.at[d, s - 1], bzr_sem.at[d, s - 1], tm, z_side(d))

    def b_far(d):
        return remote(
            ysum.at[0, pl.ds(2 * d, 2)], fb.at[d], fbs_sem.at[d], fbr_sem.at[d], tm, z_side(d, 2)
        )

    def b_stage(s):
        if s == 1:
            yb_sum(0)
            for d in range(2):
                b_far(d).start()
        for d in range(2):
            j = place(d, s)
            yb_sum(j)
            if s == 1:
                rb[d, 0] = ysum[j]
            else:
                b_copy(d, s - 1).wait_recv()
                rb[d, s - 1] += ysum[j]
            if s == 2:
                b_far(d).wait_recv()
                rb[d, 1, 2 * d : 2 * d + 2] += fb[d]
            b_copy(d, s).start()

    first = 0
    for k in range(len(blocks)):
        size = len(blocks[k])
        block = range(first, first + size)
        r = size * rows
        for j in block:
            @pl.when(jnp.logical_not(first_chip) & last_chip & (core == 1))
            def _():
                for g in range(2):
                    carry_on(j, g).wait_recv()
                    carry_back(j, g).start()

            @pl.when(jnp.logical_not(first_chip) & (core == 0))
            def _():
                for g in range(2):
                    carry_back(j, g).wait_recv()

        def enter(g, _):
            v = carry[first : first + size, g].reshape(r, n)
            hi = v.astype(BF16)
            h = times(jnp.stack([hi, (v - hi.astype(F32)).astype(BF16)]), late[g])
            hi = h.astype(BF16)
            cab[g, 0, :r] = hi
            cab[g, 1, :r] = (h - hi.astype(F32)).astype(BF16)
            return 0

        lax.fori_loop(0, 2, enter, 0)

        def month(t, dst, m):
            total = None
            for g in range(2):
                v = times(cab[g, :, :r], pre[t, g])
                for i, j in enumerate(block):
                    cum_out[t, g, chunk_rows(j), :] = v[i * rows : (i + 1) * rows]
                w = share[g] * v
                total = w if total is None else total + w
            for i, j in enumerate(block):
                dst[j, m] = total[i * rows : (i + 1) * rows]

        def b_month(m, _):
            month(m + 4, wb, m)
            return 0

        def a_month(m, _):
            month(m, wa, m)
            return 0

        for h in range(2):
            if k == 0:
                for m in (2 * h, 2 * h + 1):
                    month(m, wa, m)
                    for d in range(2):
                        a_copy(d, 1, m).start()
                    a_far(h, m % 2).start()
            else:
                lax.fori_loop(2 * h, 2 * h + 2, a_month, 0)
            lax.fori_loop(2 * h, 2 * h + 2, b_month, 0)
            for j in block:
                for o in range(1, ny):
                    yb_copy(j, h, o).start()
            if k == len(blocks) - 1 and half > 2:
                a_stage(2, (2 * h, 2 * h + 1))
        if k == 0 and ahead < 2 * nz:
            pl.when(middle)(lambda: hand_on(pieces[ahead:]))
        first += size

    for s in range(1, half - 1):
        if s > 1:
            a_stage(s + 1)
        b_stage(s)

    own_at = nz - 1
    for m in range(4):
        v = wa[own_at, m]
        for d in range(2):
            v = sum(a_come(d, half, m), v)
        wa[own_at, m] = v

    def ya_copy(o):
        src = wa.at[own_at, :, pl.ds(pl.multiple_of(y_peer(o) * sub, sub), sub), :]
        return remote(src, rya.at[o - 1], yas_sem.at[o - 1], yar_sem.at[o - 1], tm, z * ny + y_peer(o))

    for o in range(1, ny):
        ya_copy(o).start()
    b_stage(half - 1)
    for i in range(3):
        pl.when(has_next)(lambda: fwd_halo(i).wait_send())
        pl.when(has_prev)(lambda: bwd_halo(i).wait_send())
    for g in range(2):
        pl.when(core == 0)(lambda: send_t0(g).wait_send())
    for j in range(nz):
        for g in range(2):
            pl.when((core == 1) & jnp.logical_not(last_chip))(lambda: carry_on(j, g).wait_send())
            pl.when((core == 1) & jnp.logical_not(first_chip))(lambda: carry_back(j, g).wait_send())
        for o in range(1, ny):
            for h in range(2):
                yb_copy(j, h, o).wait_send()
    for d in range(2):
        b_far(d).wait_send()
        for i in range(2):
            a_far(d, i).wait_send()
        for s in range(1, half):
            b_copy(d, s).wait_send()
            for m in range(4):
                a_copy(d, s, m).wait_send()

    yb_sum(own_at)
    v = ysum[own_at]
    for d in range(2):
        b_copy(d, half - 1).wait_recv()
        v = v + rb[d, half - 1]
    pooled[4:8] = v
    if half == 2:
        for d in range(2):
            b_far(d).wait_recv()
            pooled[4 + 2 * d : 6 + 2 * d] += fb[d]
    v = wa[own_at, :, pl.ds(pl.multiple_of(y * sub, sub), sub), :]
    for o in range(1, ny):
        ya_copy(o).wait_recv()
        v = v + rya[o - 1]
    pooled[0:4] = v
    for o in range(1, ny):
        ya_copy(o).wait_send()


def deliver(cum, pooled, cum_out, pooled_out, sem):
    copies = [pltpu.make_async_copy(pooled, pooled_out, sem.at[8])]
    for i in range(8):
        part = pl.ds(i, 1)
        copies.append(pltpu.make_async_copy(cum.at[part], cum_out.at[part], sem.at[i]))
    for copy in copies:
        copy.start()
    for copy in copies:
        copy.wait()


def on_device(nz, ny, transition, entry, share):
    n = transition.shape[-1]
    half, rows = nz // 2, n // nz
    sub = rows // ny
    widest = max(len(b) for b in chunk_blocks(nz))
    dma = pltpu.SemaphoreType.DMA
    cum, pooled = pl.pallas_call(
        functools.partial(kernel, nz, ny),
        out_shape=(
            OUT(transition.shape, F32),
            OUT((8, sub, n), F32),
        ),
        in_specs=[
            pl.BlockSpec(memory_space=pltpu.HBM),
            pl.BlockSpec(memory_space=pltpu.HBM),
            pl.BlockSpec(memory_space=pltpu.HBM),
        ],
        out_specs=(pl.BlockSpec(memory_space=pltpu.VMEM), pl.BlockSpec(memory_space=pltpu.VMEM)),
        scratch_shapes=[
            pltpu.SMEM(entry.shape, entry.dtype),
            pltpu.SMEM(share.shape, F32),
            pltpu.VMEM((8, 2, n, n), F32),
            pltpu.VMEM((3, 2, n, n), F32),
            pltpu.VMEM((3, 2, n, n), F32),
            pltpu.VMEM((8, 2, 2, n, n), BF16),
            pltpu.VMEM((8, 2, 2, n, n), BF16),
            pltpu.VMEM((2, n, n), F32),
            pltpu.VMEM((2, n, n), F32),
            pltpu.VMEM((2, 2, n, n), BF16),
            pltpu.VMEM((2, n, n), F32),
            pltpu.VMEM((2, 2, n, n), BF16),
            pltpu.VMEM((nz, 2, rows, n), F32),
            pltpu.VMEM((nz, 2, rows, n), F32),
            pltpu.VMEM((2, 2, widest * rows, n), BF16),
            pltpu.VMEM((nz, 4, rows, n), F32),
            pltpu.VMEM((nz, 4, rows, n), F32),
            pltpu.VMEM((2, half - 1, 4, rows, n), F32),
            pltpu.VMEM((2, 2, rows, n), F32),
            pltpu.VMEM((2, half, 4, sub, n), F32),
            pltpu.VMEM((2, 2, sub, n), F32),
            pltpu.VMEM((ny - 1, 4, sub, n), F32),
            pltpu.VMEM((nz, ny - 1, 4, sub, n), F32),
            pltpu.VMEM((nz, 4, sub, n), F32),
            dma((2,)), dma((8,)), dma((3,)), dma((3,)), dma((3,)), dma((3,)), dma((2, 2)),
            dma((nz, 2)), dma((nz, 2)), dma((nz, 2)),
            dma((2, half - 1, 4)), dma((2, half - 1, 4)), dma((2, 2)), dma((2, 2)),
            dma((2, half - 1)), dma((2, half - 1)), dma((2,)), dma((2,)),
            dma((ny - 1,)), dma((ny - 1,)), dma((nz, 2, ny - 1)), dma((nz, 2, ny - 1)),
        ],
        compiler_params=pltpu.CompilerParams(
            collective_id=0, has_side_effects=True, vmem_limit_bytes=VMEM_LIMIT
        ),
        cost_estimate=pl.CostEstimate(
            flops=3 * 2 * 46 * n**3, bytes_accessed=2 * 4 * 16 * n * n, transcendentals=0
        ),
    )(transition, *(pltpu.with_memory_space_constraint(a, pltpu.HBM) for a in (entry, share)))
    return pl.pallas_call(
        deliver,
        out_shape=(jax.ShapeDtypeStruct(cum.shape, F32), jax.ShapeDtypeStruct(pooled.shape, F32)),
        in_specs=[pl.BlockSpec(memory_space=pltpu.VMEM)] * 2,
        out_specs=[pl.BlockSpec(memory_space=pl.ANY)] * 2,
        scratch_shapes=[dma((9,))],
        compiler_params=pltpu.CompilerParams(vmem_limit_bytes=1024 * 1024),
    )(*(pltpu.with_memory_space_constraint(a, pltpu.VMEM) for a in (cum, pooled)))


def solution(mesh, nz=8, ny=4):
    return jax.shard_map(
        functools.partial(on_device, nz, ny),
        mesh=mesh,
        in_specs=(P("tm", "cohort", None, None), P("cohort"), P("cohort")),
        out_specs=(P("tm", "cohort", None, None), P("tm", "cohort", None)),
        check_vma=False,
    )
```

```python
import functools

import jax
import jax.numpy as jnp
from jax import lax
from jax.experimental import pallas as pl
from jax.experimental.pallas import tpu as pltpu
from jax.sharding import PartitionSpec as P

MESH = pl.DeviceIdType.MESH
F32 = jnp.float32
BF16 = jnp.bfloat16
OUT = pltpu.VMEM
VMEM_LIMIT = 48 * 1024 * 1024


def chunk_blocks(nz):
    half = nz // 2
    blocks = [[d, -d] for d in range(half - 1, 0, -1)]
    blocks[0].insert(0, half)
    blocks[-1].append(0)
    return blocks


def kernel(
    nz, ny, trans, entry_in, share_in, cum_out, pooled, entry, share,
    own, hp, hn, mon, pre, t0s, t0r, late, qs, qb, carry, outc, cab, wa, wb, ra, fa, rb, fb, rya, ryb, ysum,
    in_sem, own_sem, fs_sem, bs_sem, hp_sem, hn_sem, t0_sem, cs_sem, cr_sem, cf_sem,
    as_sem, ar_sem, fas_sem, far_sem, bzs_sem, bzr_sem, fbs_sem, fbr_sem, yas_sem, yar_sem, ybs_sem, ybr_sem,
):
    n = own.shape[-1]
    half = nz // 2
    rows = n // nz
    sub = rows // ny
    blocks = chunk_blocks(nz)
    order = sum(blocks, [])
    tm = lax.axis_index("tm")
    co = lax.axis_index("cohort")
    ntm = lax.axis_size("tm")
    core, chip = lax.rem(tm, 2), tm // 2
    z, y = co // ny, lax.rem(co, ny)
    has_prev, has_next = tm > 0, tm < ntm - 1
    first_chip, last_chip = chip == 0, chip == ntm // 2 - 1

    def z_at(k):
        return lax.rem(z + nz + k, nz) * ny + y

    def y_peer(o):
        return lax.rem(y + o, ny)

    small = [pltpu.make_async_copy(entry_in, entry, in_sem.at[0]), pltpu.make_async_copy(share_in, share, in_sem.at[1])]
    for copy in small:
        copy.start()

    barrier = pltpu.get_barrier_semaphore()

    def greet(t, c):
        pl.semaphore_signal(barrier, inc=1, device_id=(t, c), device_id_type=MESH)

    near = (
        (has_prev, tm - 1), (has_next, tm + 1),
        ((core == 1) & (tm > 1), tm - 2), ((core == 1) & (tm < ntm - 2), tm + 2),
    )
    peers = 3 + ny
    for cond, t in near:
        pl.when(cond)(functools.partial(greet, t, co))
        peers = peers + jnp.where(cond, 1, 0)
    for c in [z_at(k) for k in (1, -1, 2, -2)] + [z * ny + y_peer(o) for o in range(1, ny)]:
        greet(tm, c)
    pl.semaphore_wait(barrier, peers)

    def remote(src, dst, ss, rs, t, c):
        return pltpu.make_async_remote_copy(
            src_ref=src, dst_ref=dst, send_sem=ss, recv_sem=rs, device_id=(t, c), device_id_type=MESH
        )

    def fwd_halo(i):
        return remote(trans.at[5 + i], hp.at[i], fs_sem.at[i], hp_sem.at[i], tm + 1, co)

    def bwd_halo(i):
        return remote(trans.at[i], hn.at[i], bs_sem.at[i], hn_sem.at[i], tm - 1, co)

    def own_copy(i):
        return pltpu.make_async_copy(trans.at[i], own.at[i], own_sem.at[i])

    def send_fwd():
        for i in (2, 1, 0):
            fwd_halo(i).start()

    def send_bwd():
        for i in (0, 1, 2):
            bwd_halo(i).start()

    pl.when((core == 0) & has_prev)(send_bwd)
    pl.when(has_next)(send_fwd)
    pl.when((core == 1) & has_prev)(send_bwd)

    for i in range(8):
        own_copy(i).start()

    @pl.when(jnp.logical_not(has_prev))
    def _():
        hp[...] = jnp.zeros_like(hp)

    @pl.when(jnp.logical_not(has_next))
    def _():
        hn[...] = jnp.zeros_like(hn)

    strip = min(64, n)

    def graduate(t, part=None, groups=None):
        def at(e):
            return (hp, e + 3) if e < 0 else ((hn, e - 8) if e > 7 else (own, e))

        edge = {0: 10, 1: 13, 2: 15, 5: 15, 6: 13, 7: 10}.get(t)
        scale = 1.0 / 16
        if edge is not None:
            scale = jnp.where(tm == (0 if t < 3 else ntm - 1), F32(1.0 / edge), F32(1.0 / 16))
        last, other = (t - 3, t + 3) if t == 0 else (t + 3, t - 3)
        strips = n // strip
        low = 0 if groups is None else groups[0] * strips
        high = 2 * strips if groups is None else (groups[-1] + 1) * strips

        def step(i, _):
            g, r0 = i // strips, pl.multiple_of(lax.rem(i, strips) * strip, strip)
            here = pl.ds(r0, strip)

            def load(e):
                ref, k = at(e)
                return ref[k, g, here, :]

            if groups is None:
                total = (
                    4.0 * load(t) + 3.0 * (load(t - 1) + load(t + 1))
                    + 2.0 * (load(t - 2) + load(t + 2)) + load(other)
                )
                if part is not None:
                    part[g, here, :] = total
                    return 0
            else:
                total = part[g, here, :]
            act = jnp.where(8 * tm + t >= entry[g], F32(1.0), F32(0.0))
            row = lax.broadcasted_iota(jnp.int32, (strip, n), 0) + r0
            col = lax.broadcasted_iota(jnp.int32, (strip, n), 1)
            unit = jnp.where(row == col, 1.0 - act, 0.0)
            v = (total + load(last)) * (act * scale) + unit
            hi = v.astype(BF16)
            mon[t, g, 0, here, :] = hi
            mon[t, g, 1, here, :] = (v - hi.astype(F32)).astype(BF16)
            return 0

        lax.fori_loop(low, high, step, 0)

    def dot(a, b):
        return jnp.dot(a, b, preferred_element_type=F32)

    def times(a, b):
        r = a.shape[1]
        both = dot(a.reshape(2 * r, n), b[0])
        return both[:r] + both[r:] + dot(a[0], b[1])

    def halves(ref, v):
        hi = v.astype(BF16)
        ref[0] = hi
        ref[1] = (v - hi.astype(F32)).astype(BF16)

    def multiply(dst, a, b, keep=None):
        def step(g, _):
            v = times(a(g), b(g))
            halves(dst.at[g], v)
            if keep is not None:
                keep[g] = v
            return 0
        lax.fori_loop(0, 2, step, 0)

    def take(ref, k):
        return lambda g: ref[k, g]

    def copy_pre(t):
        pre[t] = mon[t]

    def fwd_wait(i):
        pl.when(has_prev)(lambda: fwd_halo(i).wait_recv())

    def bwd_wait(i):
        pl.when(has_next)(lambda: bwd_halo(i).wait_recv())

    for copy in small:
        copy.wait()
    for i in range(8):
        own_copy(i).wait()
    graduate(3)
    graduate(4)

    def send_t0(g):
        return remote(t0s.at[g], t0r.at[g], t0_sem.at[0, g], t0_sem.at[1, g], tm + 1, co)

    def chunk(j):
        return lax.rem(z + nz + order[j], nz)

    def chunk_rows(j):
        return pl.ds(pl.multiple_of(chunk(j) * rows, rows), rows)

    def carry_on(j, g, first=False):
        src = qs.at[g, chunk_rows(j), :] if first else outc.at[j, g]
        return remote(src, carry.at[j, g], cs_sem.at[j, g], cr_sem.at[j, g], tm + 2, co)

    def carry_back(j, g):
        return remote(carry.at[j, g], carry.at[j, g], cf_sem.at[j, g], cr_sem.at[j, g], tm - 1, co)

    pieces = [(j, g) for j in range(nz) for g in range(2)]

    soon = len(blocks[0])

    def take_late(g):
        return late[g]

    @pl.when(core == 0)
    def _():
        for i in range(3):
            bwd_wait(i)
            graduate(5 + i)
        copy_pre(3)
        for t in range(4, 8):
            multiply(pre.at[t], take(pre, t - 1), take(mon, t))
        fwd_wait(2)
        graduate(2)
        fwd_wait(1)
        graduate(1)
        copy_pre(1)
        multiply(pre.at[2], take(mon, 1), take(mon, 2))
        for t in range(3, 8):
            multiply(pre.at[t], take(pre, 2), take(pre, t))
        row = lax.broadcasted_iota(jnp.int32, (n, n), 0)
        col = lax.broadcasted_iota(jnp.int32, (n, n), 1)
        for g in range(2):
            halves(pre.at[0, g], jnp.where(row == col, F32(1.0), F32(0.0)))
        graduate(0, qs)
        fwd_wait(0)
        for g in range(2):
            graduate(0, qs, [g])
            t0s[g] = times(mon[0, g], pre[7, g])
            send_t0(g).start()
        late[...] = mon[0]

    @pl.when(core == 1)
    def _():
        for i in (2, 1, 0):
            fwd_wait(i)
            graduate(i)
        copy_pre(0)
        for t in range(1, 5):
            multiply(pre.at[t], take(pre, t - 1), take(mon, t))
        for t in (5, 6):
            bwd_wait(t - 5)
            graduate(t)
            multiply(pre.at[t], take(pre, t - 1), take(mon, t))
        graduate(7, t0s)

        @pl.when(first_chip)
        def _():
            for g in range(2):
                send_t0(g).wait_recv()
                halves(late.at[g], t0r[g])
            multiply(qb, take_late, take(pre, 6))
            bwd_wait(2)
            for g in range(2):
                graduate(7, t0s, [g])
                qs[g] = times(qb[g], mon[7, g])
                for j in range(soon):
                    carry_on(j, g, True).start()
            for j in range(soon, nz):
                for g in range(2):
                    carry_on(j, g, True).start()
            multiply(pre.at[7], take(pre, 6), take(mon, 7))

        @pl.when(jnp.logical_not(first_chip))
        def _():
            bwd_wait(2)
            graduate(7, t0s, [0, 1])
            multiply(pre.at[7], take(pre, 6), take(mon, 7))
            for g in range(2):
                send_t0(g).wait_recv()
                halves(late.at[g], t0r[g])

                @pl.when(jnp.logical_not(last_chip))
                def _():
                    halves(qb.at[g], times(late[g], pre[7, g]))

    @pl.when(first_chip)
    def _():
        row = lax.broadcasted_iota(jnp.int32, (rows, n), 0)
        col = lax.broadcasted_iota(jnp.int32, (rows, n), 1)
        for j in range(nz):
            unit = jnp.where(row + chunk(j) * rows == col, F32(1.0), F32(0.0))
            for g in range(2):
                carry[j, g] = unit

    middle = jnp.logical_not(first_chip) & jnp.logical_not(last_chip) & (core == 1)

    def hand_on(some):
        for j, g in some:
            carry_on(j, g).wait_recv()
            v = carry[j, g]
            hi = v.astype(BF16)
            outc[j, g] = times(jnp.stack([hi, (v - hi.astype(F32)).astype(BF16)]), qb[g])
            carry_on(j, g).start()
            carry_back(j, g).start()

    ahead = min(2 * nz, 2 * len(blocks[0]) + 6)
    pl.when(middle)(lambda: hand_on(pieces[:ahead]))

    def place(d, s):
        return order.index(half - s if d == 0 else s - half)

    def z_side(d, k=1):
        return z_at(k if d == 0 else -k)

    def a_copy(d, s, m):
        src = wa.at[place(d, 1), m] if s == 1 else ra.at[d, s - 2, m]
        return remote(src, ra.at[d, s - 1, m], as_sem.at[d, s - 1, m], ar_sem.at[d, s - 1, m], tm, z_side(d))

    def a_far(d, i):
        return remote(wa.at[0, 2 * d + i], fa.at[d, i], fas_sem.at[d, i], far_sem.at[d, i], tm, z_side(d, 2))

    def a_come(d, s, m):
        parts = []
        if s >= 2:
            a_copy(d, s - 1, m).wait_recv()
            parts.append(ra[d, s - 2, m])
        if s == 2 and m // 2 == d:
            a_far(d, m % 2).wait_recv()
            parts.append(fa[d, m % 2])
        return parts

    def a_stage(s, months=range(4)):
        for m in months:
            for d in range(2):
                ra[d, s - 2, m] = sum(a_come(d, s, m), wa[place(d, s), m])
                a_copy(d, s, m).start()

    def yb_copy(j, h, o):
        rows_to = pl.ds(pl.multiple_of(y_peer(o) * sub, sub), sub)
        return remote(
            wb.at[j, pl.ds(2 * h, 2), rows_to, :], ryb.at[j, o - 1, pl.ds(2 * h, 2)],
            ybs_sem.at[j, h, o - 1], ybr_sem.at[j, h, o - 1], tm, z * ny + y_peer(o),
        )

    summed = set()

    def yb_sum(j):
        if j not in summed:
            summed.add(j)
            v = wb[j, :, pl.ds(pl.multiple_of(y * sub, sub), sub), :]
            for o in range(1, ny):
                for h in range(2):
                    yb_copy(j, h, o).wait_recv()
                v = v + ryb[j, o - 1]
            ysum[j] = v

    def b_copy(d, s):
        return remote(rb.at[d, s - 1], rb.at[d, s], bzs_sem.at[d, s - 1], bzr_sem.at[d, s - 1], tm, z_side(d))

    def b_far(d):
        return remote(
            ysum.at[0, pl.ds(2 * d, 2)], fb.at[d], fbs_sem.at[d], fbr_sem.at[d], tm, z_side(d, 2)
        )

    def b_stage(s):
        if s == 1:
            yb_sum(0)
            for d in range(2):
                b_far(d).start()
        for d in range(2):
            j = place(d, s)
            yb_sum(j)
            if s == 1:
                rb[d, 0] = ysum[j]
            else:
                b_copy(d, s - 1).wait_recv()
                rb[d, s - 1] += ysum[j]
            if s == 2:
                b_far(d).wait_recv()
                rb[d, 1, 2 * d : 2 * d + 2] += fb[d]
            b_copy(d, s).start()

    first = 0
    for k in range(len(blocks)):
        size = len(blocks[k])
        block = range(first, first + size)
        r = size * rows
        for j in block:
            @pl.when(jnp.logical_not(first_chip) & last_chip & (core == 1))
            def _():
                for g in range(2):
                    carry_on(j, g).wait_recv()
                    carry_back(j, g).start()

            @pl.when(jnp.logical_not(first_chip) & (core == 0))
            def _():
                for g in range(2):
                    carry_back(j, g).wait_recv()

        def enter(g, _):
            v = carry[first : first + size, g].reshape(r, n)
            hi = v.astype(BF16)
            h = times(jnp.stack([hi, (v - hi.astype(F32)).astype(BF16)]), late[g])
            hi = h.astype(BF16)
            cab[g, 0, :r] = hi
            cab[g, 1, :r] = (h - hi.astype(F32)).astype(BF16)
            return 0

        lax.fori_loop(0, 2, enter, 0)

        def month(t, dst, m):
            total = None
            for g in range(2):
                v = times(cab[g, :, :r], pre[t, g])
                for i, j in enumerate(block):
                    cum_out[t, g, chunk_rows(j), :] = v[i * rows : (i + 1) * rows]
                w = share[g] * v
                total = w if total is None else total + w
            for i, j in enumerate(block):
                dst[j, m] = total[i * rows : (i + 1) * rows]

        def b_month(m, _):
            month(m + 4, wb, m)
            return 0

        def a_month(m, _):
            month(m, wa, m)
            return 0

        if k == len(blocks) - 1 and half > 2:
            a_stage(2, (0, 1))
        for h in range(2):
            if k == 0:
                for m in (2 * h, 2 * h + 1):
                    month(m, wa, m)
                    for d in range(2):
                        a_copy(d, 1, m).start()
                    a_far(h, m % 2).start()
            else:
                lax.fori_loop(2 * h, 2 * h + 2, a_month, 0)
            lax.fori_loop(2 * h, 2 * h + 2, b_month, 0)
            for j in block:
                for o in range(1, ny):
                    yb_copy(j, h, o).start()
            if k == len(blocks) - 1 and half > 2 and h == 0:
                a_stage(2, (2, 3))
        if k == 0 and ahead < 2 * nz:
            pl.when(middle)(lambda: hand_on(pieces[ahead:]))
        first += size

    for s in range(1, half - 1):
        if s > 1:
            a_stage(s + 1)
        b_stage(s)

    own_at = nz - 1
    for m in range(4):
        v = wa[own_at, m]
        for d in range(2):
            v = sum(a_come(d, half, m), v)
        wa[own_at, m] = v

    def ya_copy(o):
        src = wa.at[own_at, :, pl.ds(pl.multiple_of(y_peer(o) * sub, sub), sub), :]
        return remote(src, rya.at[o - 1], yas_sem.at[o - 1], yar_sem.at[o - 1], tm, z * ny + y_peer(o))

    for o in range(1, ny):
        ya_copy(o).start()
    b_stage(half - 1)
    for i in range(3):
        pl.when(has_next)(lambda: fwd_halo(i).wait_send())
        pl.when(has_prev)(lambda: bwd_halo(i).wait_send())
    for g in range(2):
        pl.when(core == 0)(lambda: send_t0(g).wait_send())
    for j in range(nz):
        for g in range(2):
            pl.when((core == 1) & jnp.logical_not(last_chip))(lambda: carry_on(j, g).wait_send())
            pl.when((core == 1) & jnp.logical_not(first_chip))(lambda: carry_back(j, g).wait_send())
        for o in range(1, ny):
            for h in range(2):
                yb_copy(j, h, o).wait_send()
    for d in range(2):
        b_far(d).wait_send()
        for i in range(2):
            a_far(d, i).wait_send()
        for s in range(1, half):
            b_copy(d, s).wait_send()
            for m in range(4):
                a_copy(d, s, m).wait_send()

    yb_sum(own_at)
    v = ysum[own_at]
    for d in range(2):
        b_copy(d, half - 1).wait_recv()
        v = v + rb[d, half - 1]
    pooled[4:8] = v
    if half == 2:
        for d in range(2):
            b_far(d).wait_recv()
            pooled[4 + 2 * d : 6 + 2 * d] += fb[d]
    v = wa[own_at, :, pl.ds(pl.multiple_of(y * sub, sub), sub), :]
    for o in range(1, ny):
        ya_copy(o).wait_recv()
        v = v + rya[o - 1]
    pooled[0:4] = v
    for o in range(1, ny):
        ya_copy(o).wait_send()


def deliver(cum, pooled, cum_out, pooled_out, sem):
    copies = [pltpu.make_async_copy(pooled, pooled_out, sem.at[8])]
    for i in range(8):
        part = pl.ds(i, 1)
        copies.append(pltpu.make_async_copy(cum.at[part], cum_out.at[part], sem.at[i]))
    for copy in copies:
        copy.start()
    for copy in copies:
        copy.wait()


def on_device(nz, ny, transition, entry, share):
    n = transition.shape[-1]
    half, rows = nz // 2, n // nz
    sub = rows // ny
    widest = max(len(b) for b in chunk_blocks(nz))
    dma = pltpu.SemaphoreType.DMA
    cum, pooled = pl.pallas_call(
        functools.partial(kernel, nz, ny),
        out_shape=(
            OUT(transition.shape, F32),
            OUT((8, sub, n), F32),
        ),
        in_specs=[
            pl.BlockSpec(memory_space=pltpu.HBM),
            pl.BlockSpec(memory_space=pltpu.HBM),
            pl.BlockSpec(memory_space=pltpu.HBM),
        ],
        out_specs=(pl.BlockSpec(memory_space=pltpu.VMEM), pl.BlockSpec(memory_space=pltpu.VMEM)),
        scratch_shapes=[
            pltpu.SMEM(entry.shape, entry.dtype),
            pltpu.SMEM(share.shape, F32),
            pltpu.VMEM((8, 2, n, n), F32),
            pltpu.VMEM((3, 2, n, n), F32),
            pltpu.VMEM((3, 2, n, n), F32),
            pltpu.VMEM((8, 2, 2, n, n), BF16),
            pltpu.VMEM((8, 2, 2, n, n), BF16),
            pltpu.VMEM((2, n, n), F32),
            pltpu.VMEM((2, n, n), F32),
            pltpu.VMEM((2, 2, n, n), BF16),
            pltpu.VMEM((2, n, n), F32),
            pltpu.VMEM((2, 2, n, n), BF16),
            pltpu.VMEM((nz, 2, rows, n), F32),
            pltpu.VMEM((nz, 2, rows, n), F32),
            pltpu.VMEM((2, 2, widest * rows, n), BF16),
            pltpu.VMEM((nz, 4, rows, n), F32),
            pltpu.VMEM((nz, 4, rows, n), F32),
            pltpu.VMEM((2, half - 1, 4, rows, n), F32),
            pltpu.VMEM((2, 2, rows, n), F32),
            pltpu.VMEM((2, half, 4, sub, n), F32),
            pltpu.VMEM((2, 2, sub, n), F32),
            pltpu.VMEM((ny - 1, 4, sub, n), F32),
            pltpu.VMEM((nz, ny - 1, 4, sub, n), F32),
            pltpu.VMEM((nz, 4, sub, n), F32),
            dma((2,)), dma((8,)), dma((3,)), dma((3,)), dma((3,)), dma((3,)), dma((2, 2)),
            dma((nz, 2)), dma((nz, 2)), dma((nz, 2)),
            dma((2, half - 1, 4)), dma((2, half - 1, 4)), dma((2, 2)), dma((2, 2)),
            dma((2, half - 1)), dma((2, half - 1)), dma((2,)), dma((2,)),
            dma((ny - 1,)), dma((ny - 1,)), dma((nz, 2, ny - 1)), dma((nz, 2, ny - 1)),
        ],
        compiler_params=pltpu.CompilerParams(
            collective_id=0, has_side_effects=True, vmem_limit_bytes=VMEM_LIMIT
        ),
        cost_estimate=pl.CostEstimate(
            flops=3 * 2 * 46 * n**3, bytes_accessed=2 * 4 * 16 * n * n, transcendentals=0
        ),
    )(transition, *(pltpu.with_memory_space_constraint(a, pltpu.HBM) for a in (entry, share)))
    return pl.pallas_call(
        deliver,
        out_shape=(jax.ShapeDtypeStruct(cum.shape, F32), jax.ShapeDtypeStruct(pooled.shape, F32)),
        in_specs=[pl.BlockSpec(memory_space=pltpu.VMEM)] * 2,
        out_specs=[pl.BlockSpec(memory_space=pl.ANY)] * 2,
        scratch_shapes=[dma((9,))],
        compiler_params=pltpu.CompilerParams(vmem_limit_bytes=1024 * 1024),
    )(*(pltpu.with_memory_space_constraint(a, pltpu.VMEM) for a in (cum, pooled)))


def solution(mesh, nz=8, ny=4):
    return jax.shard_map(
        functools.partial(on_device, nz, ny),
        mesh=mesh,
        in_specs=(P("tm", "cohort", None, None), P("cohort"), P("cohort")),
        out_specs=(P("tm", "cohort", None, None), P("tm", "cohort", None)),
        check_vma=False,
    )
```

```python
import functools

import jax
import jax.numpy as jnp
from jax import lax
from jax.experimental import pallas as pl
from jax.experimental.pallas import tpu as pltpu
from jax.sharding import PartitionSpec as P

MESH = pl.DeviceIdType.MESH
F32 = jnp.float32
BF16 = jnp.bfloat16
OUT = pltpu.VMEM
VMEM_LIMIT = 48 * 1024 * 1024


def chunk_blocks(nz):
    half = nz // 2
    blocks = [[d, -d] for d in range(half - 1, 0, -1)]
    blocks[0].insert(0, half)
    blocks[-1].append(0)
    return blocks


def kernel(
    nz, ny, trans, entry_in, share_in, cum_out, pooled, entry, share,
    own, hp, hn, mon, pre, t0s, t0r, late, qs, qb, carry, outc, cab, wa, wb, ra, fa, rb, fb, rya, ryb, ysum,
    in_sem, own_sem, fs_sem, bs_sem, hp_sem, hn_sem, t0_sem, cs_sem, cr_sem, cf_sem,
    as_sem, ar_sem, fas_sem, far_sem, bzs_sem, bzr_sem, fbs_sem, fbr_sem, yas_sem, yar_sem, ybs_sem, ybr_sem,
):
    n = own.shape[-1]
    half = nz // 2
    rows = n // nz
    sub = rows // ny
    blocks = chunk_blocks(nz)
    order = sum(blocks, [])
    tm = lax.axis_index("tm")
    co = lax.axis_index("cohort")
    ntm = lax.axis_size("tm")
    core, chip = lax.rem(tm, 2), tm // 2
    z, y = co // ny, lax.rem(co, ny)
    has_prev, has_next = tm > 0, tm < ntm - 1
    first_chip, last_chip = chip == 0, chip == ntm // 2 - 1

    def z_at(k):
        return lax.rem(z + nz + k, nz) * ny + y

    def y_peer(o):
        return lax.rem(y + o, ny)

    small = [pltpu.make_async_copy(entry_in, entry, in_sem.at[0]), pltpu.make_async_copy(share_in, share, in_sem.at[1])]
    for copy in small:
        copy.start()

    barrier = pltpu.get_barrier_semaphore()

    def greet(t, c):
        pl.semaphore_signal(barrier, inc=1, device_id=(t, c), device_id_type=MESH)

    near = (
        (has_prev, tm - 1), (has_next, tm + 1),
        ((core == 1) & (tm > 1), tm - 2), ((core == 1) & (tm < ntm - 2), tm + 2),
    )
    peers = 3 + ny
    for cond, t in near:
        pl.when(cond)(functools.partial(greet, t, co))
        peers = peers + jnp.where(cond, 1, 0)
    for c in [z_at(k) for k in (1, -1, 2, -2)] + [z * ny + y_peer(o) for o in range(1, ny)]:
        greet(tm, c)
    pl.semaphore_wait(barrier, peers)

    def remote(src, dst, ss, rs, t, c):
        return pltpu.make_async_remote_copy(
            src_ref=src, dst_ref=dst, send_sem=ss, recv_sem=rs, device_id=(t, c), device_id_type=MESH
        )

    def fwd_halo(i, g):
        return remote(trans.at[5 + i, g], hp.at[i, g], fs_sem.at[i, g], hp_sem.at[i, g], tm + 1, co)

    def bwd_halo(i, g):
        return remote(trans.at[i, g], hn.at[i, g], bs_sem.at[i, g], hn_sem.at[i, g], tm - 1, co)

    def own_copy(i):
        return pltpu.make_async_copy(trans.at[i], own.at[i], own_sem.at[i])

    def send_fwd():
        for i in (2, 1, 0):
            for g in range(2):
                fwd_halo(i, g).start()

    def send_bwd():
        for i in (0, 1, 2):
            for g in range(2):
                bwd_halo(i, g).start()

    pl.when((core == 0) & has_prev)(send_bwd)
    pl.when(has_next)(send_fwd)
    pl.when((core == 1) & has_prev)(send_bwd)

    for i in range(8):
        own_copy(i).start()

    @pl.when(jnp.logical_not(has_prev))
    def _():
        hp[...] = jnp.zeros_like(hp)

    @pl.when(jnp.logical_not(has_next))
    def _():
        hn[...] = jnp.zeros_like(hn)

    strip = min(64, n)

    def graduate(t, part=None, groups=None):
        def at(e):
            return (hp, e + 3) if e < 0 else ((hn, e - 8) if e > 7 else (own, e))

        edge = {0: 10, 1: 13, 2: 15, 5: 15, 6: 13, 7: 10}.get(t)
        scale = 1.0 / 16
        if edge is not None:
            scale = jnp.where(tm == (0 if t < 3 else ntm - 1), F32(1.0 / edge), F32(1.0 / 16))
        last, other = (t - 3, t + 3) if t == 0 else (t + 3, t - 3)
        strips = n // strip
        low = 0 if groups is None else groups[0] * strips
        high = 2 * strips if groups is None else (groups[-1] + 1) * strips

        def step(i, _):
            g, r0 = i // strips, pl.multiple_of(lax.rem(i, strips) * strip, strip)
            here = pl.ds(r0, strip)

            def load(e):
                ref, k = at(e)
                return ref[k, g, here, :]

            if groups is None:
                total = (
                    4.0 * load(t) + 3.0 * (load(t - 1) + load(t + 1))
                    + 2.0 * (load(t - 2) + load(t + 2)) + load(other)
                )
                if part is not None:
                    part[g, here, :] = total
                    return 0
            else:
                total = part[g, here, :]
            act = jnp.where(8 * tm + t >= entry[g], F32(1.0), F32(0.0))
            row = lax.broadcasted_iota(jnp.int32, (strip, n), 0) + r0
            col = lax.broadcasted_iota(jnp.int32, (strip, n), 1)
            unit = jnp.where(row == col, 1.0 - act, 0.0)
            v = (total + load(last)) * (act * scale) + unit
            hi = v.astype(BF16)
            mon[t, g, 0, here, :] = hi
            mon[t, g, 1, here, :] = (v - hi.astype(F32)).astype(BF16)
            return 0

        lax.fori_loop(low, high, step, 0)

    def dot(a, b):
        return jnp.dot(a, b, preferred_element_type=F32)

    def times(a, b):
        r = a.shape[1]
        both = dot(a.reshape(2 * r, n), b[0])
        return both[:r] + both[r:] + dot(a[0], b[1])

    def halves(ref, v):
        hi = v.astype(BF16)
        ref[0] = hi
        ref[1] = (v - hi.astype(F32)).astype(BF16)

    def multiply(dst, a, b, keep=None):
        def step(g, _):
            v = times(a(g), b(g))
            halves(dst.at[g], v)
            if keep is not None:
                keep[g] = v
            return 0
        lax.fori_loop(0, 2, step, 0)

    def take(ref, k):
        return lambda g: ref[k, g]

    def copy_pre(t):
        pre[t] = mon[t]

    def fwd_wait(i, groups=(0, 1)):
        for g in groups:
            pl.when(has_prev)(lambda: fwd_halo(i, g).wait_recv())

    def bwd_wait(i, groups=(0, 1)):
        for g in groups:
            pl.when(has_next)(lambda: bwd_halo(i, g).wait_recv())

    for copy in small:
        copy.wait()
    for i in range(8):
        own_copy(i).wait()
    graduate(3)
    graduate(4)

    def send_t0(g):
        return remote(t0s.at[g], t0r.at[g], t0_sem.at[0, g], t0_sem.at[1, g], tm + 1, co)

    def chunk(j):
        return lax.rem(z + nz + order[j], nz)

    def chunk_rows(j):
        return pl.ds(pl.multiple_of(chunk(j) * rows, rows), rows)

    def carry_on(j, g, first=False):
        src = qs.at[g, chunk_rows(j), :] if first else outc.at[j, g]
        return remote(src, carry.at[j, g], cs_sem.at[j, g], cr_sem.at[j, g], tm + 2, co)

    def carry_back(j, g):
        return remote(carry.at[j, g], carry.at[j, g], cf_sem.at[j, g], cr_sem.at[j, g], tm - 1, co)

    pieces = [(j, g) for j in range(nz) for g in range(2)]

    soon = len(blocks[0])

    def take_late(g):
        return late[g]

    @pl.when(core == 0)
    def _():
        for i in range(3):
            bwd_wait(i)
            graduate(5 + i)
        copy_pre(3)
        for t in range(4, 8):
            multiply(pre.at[t], take(pre, t - 1), take(mon, t))
        fwd_wait(2)
        graduate(2)
        fwd_wait(1)
        graduate(1)
        copy_pre(1)
        multiply(pre.at[2], take(mon, 1), take(mon, 2))
        for t in range(3, 8):
            multiply(pre.at[t], take(pre, 2), take(pre, t))
        row = lax.broadcasted_iota(jnp.int32, (n, n), 0)
        col = lax.broadcasted_iota(jnp.int32, (n, n), 1)
        for g in range(2):
            halves(pre.at[0, g], jnp.where(row == col, F32(1.0), F32(0.0)))
        graduate(0, qs)
        for g in range(2):
            fwd_wait(0, [g])
            graduate(0, qs, [g])
            t0s[g] = times(mon[0, g], pre[7, g])
            send_t0(g).start()
        late[...] = mon[0]

    @pl.when(core == 1)
    def _():
        for i in (2, 1, 0):
            fwd_wait(i)
            graduate(i)
        copy_pre(0)
        for t in range(1, 5):
            multiply(pre.at[t], take(pre, t - 1), take(mon, t))
        for t in (5, 6):
            bwd_wait(t - 5)
            graduate(t)
            multiply(pre.at[t], take(pre, t - 1), take(mon, t))
        graduate(7, t0s)

        @pl.when(first_chip)
        def _():
            for g in range(2):
                send_t0(g).wait_recv()
                halves(late.at[g], t0r[g])
            multiply(qb, take_late, take(pre, 6))
            bwd_wait(2, [0])
            graduate(7, t0s, [0])
            qs[0] = times(qb[0], mon[7, 0])
            bwd_wait(2, [1])
            for j in range(soon):
                carry_on(j, 0, True).start()
            graduate(7, t0s, [1])
            qs[1] = times(qb[1], mon[7, 1])
            for j in range(soon):
                carry_on(j, 1, True).start()
            for j in range(soon, nz):
                for g in range(2):
                    carry_on(j, g, True).start()
            multiply(pre.at[7], take(pre, 6), take(mon, 7))

        @pl.when(jnp.logical_not(first_chip))
        def _():
            for g in range(2):
                bwd_wait(2, [g])
                graduate(7, t0s, [g])
                halves(pre.at[7, g], times(pre[6, g], mon[7, g]))
            for g in range(2):
                send_t0(g).wait_recv()
                halves(late.at[g], t0r[g])

                @pl.when(jnp.logical_not(last_chip))
                def _():
                    halves(qb.at[g], times(late[g], pre[7, g]))

    @pl.when(first_chip)
    def _():
        row = lax.broadcasted_iota(jnp.int32, (rows, n), 0)
        col = lax.broadcasted_iota(jnp.int32, (rows, n), 1)
        for j in range(nz):
            unit = jnp.where(row + chunk(j) * rows == col, F32(1.0), F32(0.0))
            for g in range(2):
                carry[j, g] = unit

    middle = jnp.logical_not(first_chip) & jnp.logical_not(last_chip) & (core == 1)

    def hand_on(some):
        for j, g in some:
            carry_on(j, g).wait_recv()
            v = carry[j, g]
            hi = v.astype(BF16)
            outc[j, g] = times(jnp.stack([hi, (v - hi.astype(F32)).astype(BF16)]), qb[g])
            carry_on(j, g).start()
            carry_back(j, g).start()

    ahead = min(2 * nz, 2 * len(blocks[0]) + 10)
    pl.when(middle)(lambda: hand_on(pieces[:ahead]))

    def place(d, s):
        return order.index(half - s if d == 0 else s - half)

    def z_side(d, k=1):
        return z_at(k if d == 0 else -k)

    def a_copy(d, s, m):
        src = wa.at[place(d, 1), m] if s == 1 else ra.at[d, s - 2, m]
        return remote(src, ra.at[d, s - 1, m], as_sem.at[d, s - 1, m], ar_sem.at[d, s - 1, m], tm, z_side(d))

    def a_far(d, i):
        return remote(wa.at[0, 2 * d + i], fa.at[d, i], fas_sem.at[d, i], far_sem.at[d, i], tm, z_side(d, 2))

    def a_come(d, s, m):
        parts = []
        if s >= 2:
            a_copy(d, s - 1, m).wait_recv()
            parts.append(ra[d, s - 2, m])
        if s == 2 and m // 2 == d:
            a_far(d, m % 2).wait_recv()
            parts.append(fa[d, m % 2])
        return parts

    def a_stage(s, months=range(4)):
        for m in months:
            for d in range(2):
                ra[d, s - 2, m] = sum(a_come(d, s, m), wa[place(d, s), m])
                a_copy(d, s, m).start()

    def yb_copy(j, h, o):
        rows_to = pl.ds(pl.multiple_of(y_peer(o) * sub, sub), sub)
        return remote(
            wb.at[j, pl.ds(2 * h, 2), rows_to, :], ryb.at[j, o - 1, pl.ds(2 * h, 2)],
            ybs_sem.at[j, h, o - 1], ybr_sem.at[j, h, o - 1], tm, z * ny + y_peer(o),
        )

    summed = set()

    def yb_sum(j):
        if j not in summed:
            summed.add(j)
            v = wb[j, :, pl.ds(pl.multiple_of(y * sub, sub), sub), :]
            for o in range(1, ny):
                for h in range(2):
                    yb_copy(j, h, o).wait_recv()
                v = v + ryb[j, o - 1]
            ysum[j] = v

    def b_copy(d, s):
        return remote(rb.at[d, s - 1], rb.at[d, s], bzs_sem.at[d, s - 1], bzr_sem.at[d, s - 1], tm, z_side(d))

    def b_far(d):
        return remote(
            ysum.at[0, pl.ds(2 * d, 2)], fb.at[d], fbs_sem.at[d], fbr_sem.at[d], tm, z_side(d, 2)
        )

    def b_stage(s):
        if s == 1:
            yb_sum(0)
            for d in range(2):
                b_far(d).start()
        for d in range(2):
            j = place(d, s)
            yb_sum(j)
            if s == 1:
                rb[d, 0] = ysum[j]
            else:
                b_copy(d, s - 1).wait_recv()
                rb[d, s - 1] += ysum[j]
            if s == 2:
                b_far(d).wait_recv()
                rb[d, 1, 2 * d : 2 * d + 2] += fb[d]
            b_copy(d, s).start()

    first = 0
    for k in range(len(blocks)):
        size = len(blocks[k])
        block = range(first, first + size)
        r = size * rows
        for j in block:
            @pl.when(jnp.logical_not(first_chip) & last_chip & (core == 1))
            def _():
                for g in range(2):
                    carry_on(j, g).wait_recv()
                    carry_back(j, g).start()

            @pl.when(jnp.logical_not(first_chip) & (core == 0))
            def _():
                for g in range(2):
                    carry_back(j, g).wait_recv()

        def enter(g, _):
            v = carry[first : first + size, g].reshape(r, n)
            hi = v.astype(BF16)
            h = times(jnp.stack([hi, (v - hi.astype(F32)).astype(BF16)]), late[g])
            hi = h.astype(BF16)
            cab[g, 0, :r] = hi
            cab[g, 1, :r] = (h - hi.astype(F32)).astype(BF16)
            return 0

        lax.fori_loop(0, 2, enter, 0)

        def month(t, dst, m):
            total = None
            for g in range(2):
                v = times(cab[g, :, :r], pre[t, g])
                for i, j in enumerate(block):
                    cum_out[t, g, chunk_rows(j), :] = v[i * rows : (i + 1) * rows]
                w = share[g] * v
                total = w if total is None else total + w
            for i, j in enumerate(block):
                dst[j, m] = total[i * rows : (i + 1) * rows]

        def b_month(m, _):
            month(m + 4, wb, m)
            return 0

        def a_month(m, _):
            month(m, wa, m)
            return 0

        if k == len(blocks) - 1 and half > 2:
            a_stage(2, (0, 1))
        for h in range(2):
            if k == 0:
                for m in (2 * h, 2 * h + 1):
                    month(m, wa, m)
                    for d in range(2):
                        a_copy(d, 1, m).start()
                    a_far(h, m % 2).start()
            else:
                lax.fori_loop(2 * h, 2 * h + 2, a_month, 0)
            lax.fori_loop(2 * h, 2 * h + 2, b_month, 0)
            for j in block:
                for o in range(1, ny):
                    yb_copy(j, h, o).start()
            if k == len(blocks) - 1 and half > 2 and h == 0:
                a_stage(2, (2, 3))
                b_stage(1)
        if k == 0 and ahead < 2 * nz:
            pl.when(middle)(lambda: hand_on(pieces[ahead:]))
        first += size

    for s in range(1, half - 1):
        if s > 1:
            a_stage(s + 1)
            b_stage(s)

    own_at = nz - 1
    for m in range(4):
        v = wa[own_at, m]
        for d in range(2):
            v = sum(a_come(d, half, m), v)
        wa[own_at, m] = v

    def ya_copy(o):
        src = wa.at[own_at, :, pl.ds(pl.multiple_of(y_peer(o) * sub, sub), sub), :]
        return remote(src, rya.at[o - 1], yas_sem.at[o - 1], yar_sem.at[o - 1], tm, z * ny + y_peer(o))

    for o in range(1, ny):
        ya_copy(o).start()
    b_stage(half - 1)
    for i in range(3):
        for g in range(2):
            pl.when(has_next)(lambda: fwd_halo(i, g).wait_send())
            pl.when(has_prev)(lambda: bwd_halo(i, g).wait_send())
    for g in range(2):
        pl.when(core == 0)(lambda: send_t0(g).wait_send())
    for j in range(nz):
        for g in range(2):
            pl.when((core == 1) & jnp.logical_not(last_chip))(lambda: carry_on(j, g).wait_send())
            pl.when((core == 1) & jnp.logical_not(first_chip))(lambda: carry_back(j, g).wait_send())
        for o in range(1, ny):
            for h in range(2):
                yb_copy(j, h, o).wait_send()
    for d in range(2):
        b_far(d).wait_send()
        for i in range(2):
            a_far(d, i).wait_send()
        for s in range(1, half):
            b_copy(d, s).wait_send()
            for m in range(4):
                a_copy(d, s, m).wait_send()

    yb_sum(own_at)
    v = ysum[own_at]
    for d in range(2):
        b_copy(d, half - 1).wait_recv()
        v = v + rb[d, half - 1]
    pooled[4:8] = v
    if half == 2:
        for d in range(2):
            b_far(d).wait_recv()
            pooled[4 + 2 * d : 6 + 2 * d] += fb[d]
    v = wa[own_at, :, pl.ds(pl.multiple_of(y * sub, sub), sub), :]
    for o in range(1, ny):
        ya_copy(o).wait_recv()
        v = v + rya[o - 1]
    pooled[0:4] = v
    for o in range(1, ny):
        ya_copy(o).wait_send()


def deliver(cum, pooled, cum_out, pooled_out, sem):
    copies = [pltpu.make_async_copy(pooled, pooled_out, sem.at[8])]
    for i in range(8):
        part = pl.ds(i, 1)
        copies.append(pltpu.make_async_copy(cum.at[part], cum_out.at[part], sem.at[i]))
    for copy in copies:
        copy.start()
    for copy in copies:
        copy.wait()


def on_device(nz, ny, transition, entry, share):
    n = transition.shape[-1]
    half, rows = nz // 2, n // nz
    sub = rows // ny
    widest = max(len(b) for b in chunk_blocks(nz))
    dma = pltpu.SemaphoreType.DMA
    cum, pooled = pl.pallas_call(
        functools.partial(kernel, nz, ny),
        out_shape=(
            OUT(transition.shape, F32),
            OUT((8, sub, n), F32),
        ),
        in_specs=[
            pl.BlockSpec(memory_space=pltpu.HBM),
            pl.BlockSpec(memory_space=pltpu.HBM),
            pl.BlockSpec(memory_space=pltpu.HBM),
        ],
        out_specs=(pl.BlockSpec(memory_space=pltpu.VMEM), pl.BlockSpec(memory_space=pltpu.VMEM)),
        scratch_shapes=[
            pltpu.SMEM(entry.shape, entry.dtype),
            pltpu.SMEM(share.shape, F32),
            pltpu.VMEM((8, 2, n, n), F32),
            pltpu.VMEM((3, 2, n, n), F32),
            pltpu.VMEM((3, 2, n, n), F32),
            pltpu.VMEM((8, 2, 2, n, n), BF16),
            pltpu.VMEM((8, 2, 2, n, n), BF16),
            pltpu.VMEM((2, n, n), F32),
            pltpu.VMEM((2, n, n), F32),
            pltpu.VMEM((2, 2, n, n), BF16),
            pltpu.VMEM((2, n, n), F32),
            pltpu.VMEM((2, 2, n, n), BF16),
            pltpu.VMEM((nz, 2, rows, n), F32),
            pltpu.VMEM((nz, 2, rows, n), F32),
            pltpu.VMEM((2, 2, widest * rows, n), BF16),
            pltpu.VMEM((nz, 4, rows, n), F32),
            pltpu.VMEM((nz, 4, rows, n), F32),
            pltpu.VMEM((2, half - 1, 4, rows, n), F32),
            pltpu.VMEM((2, 2, rows, n), F32),
            pltpu.VMEM((2, half, 4, sub, n), F32),
            pltpu.VMEM((2, 2, sub, n), F32),
            pltpu.VMEM((ny - 1, 4, sub, n), F32),
            pltpu.VMEM((nz, ny - 1, 4, sub, n), F32),
            pltpu.VMEM((nz, 4, sub, n), F32),
            dma((2,)), dma((8,)), dma((3, 2)), dma((3, 2)), dma((3, 2)), dma((3, 2)), dma((2, 2)),
            dma((nz, 2)), dma((nz, 2)), dma((nz, 2)),
            dma((2, half - 1, 4)), dma((2, half - 1, 4)), dma((2, 2)), dma((2, 2)),
            dma((2, half - 1)), dma((2, half - 1)), dma((2,)), dma((2,)),
            dma((ny - 1,)), dma((ny - 1,)), dma((nz, 2, ny - 1)), dma((nz, 2, ny - 1)),
        ],
        compiler_params=pltpu.CompilerParams(
            collective_id=0, has_side_effects=True, vmem_limit_bytes=VMEM_LIMIT
        ),
        cost_estimate=pl.CostEstimate(
            flops=3 * 2 * 46 * n**3, bytes_accessed=2 * 4 * 16 * n * n, transcendentals=0
        ),
    )(transition, *(pltpu.with_memory_space_constraint(a, pltpu.HBM) for a in (entry, share)))
    return pl.pallas_call(
        deliver,
        out_shape=(jax.ShapeDtypeStruct(cum.shape, F32), jax.ShapeDtypeStruct(pooled.shape, F32)),
        in_specs=[pl.BlockSpec(memory_space=pltpu.VMEM)] * 2,
        out_specs=[pl.BlockSpec(memory_space=pl.ANY)] * 2,
        scratch_shapes=[dma((9,))],
        compiler_params=pltpu.CompilerParams(vmem_limit_bytes=1024 * 1024),
    )(*(pltpu.with_memory_space_constraint(a, pltpu.VMEM) for a in (cum, pooled)))


def solution(mesh, nz=8, ny=4):
    return jax.shard_map(
        functools.partial(on_device, nz, ny),
        mesh=mesh,
        in_specs=(P("tm", "cohort", None, None), P("cohort"), P("cohort")),
        out_specs=(P("tm", "cohort", None, None), P("tm", "cohort", None)),
        check_vma=False,
    )
```
